512 devices in a mesh: space: 64 (over z, y), rep: 8 (over x, core).
Axes of the slice: x: 4, y: 8, z: 8, core: 2. Of those that a mesh axis runs over, the one named last changes fastest.
Arguments:
- features: bfloat16 [8, 256, 96, 512], P('rep', 'space'), may hold values from -6 to 6
- occupancy: int32 [8, 256, 512], P('rep', 'space'), may hold values from 0 to 1, as said below
- neighbours: int32 [8, 256, 27], P('rep', 'space'), may hold values from 0 to 12, as said below
- owners: int32 [8, 256], P('rep', 'space'), may hold values from 0 to 63, as said below
- octslots: int32 [8, 256], P('rep', 'space'), may hold values from 0 to 15, as said below
- cotangent: bfloat16 [8, 128, 128, 512], P('rep', 'space'), may hold values from -0.046875 to 0.046875
- w_sub: bfloat16 [27, 96, 96], replicated, may hold values from -0.125 to 0.125
- w_down: bfloat16 [8, 128, 96], replicated, may hold values from -0.21875 to 0.21875
Outputs:
- coarse: bfloat16 [8, 128, 128, 512], P('rep', 'space')
- grad_sub: float32 [27, 96, 96], replicated
- grad_down: float32 [8, 128, 96], replicated
The draws below stay inside these ranges and needn't reach their ends.
Inputs may be any that keep to these rules, and one draw needn't show every extreme that they name: `occupancy`: zero on every voxel of a slot past its device's count of active bricks; some device of each tile has all 4 slots active. `neighbours`: code n of offset (dx, dy, dz) is 12 or (dx + 1) * 4 + s, where s is the slot of an active brick on the space device dx away; the map has no bricks beyond its first and last space device; inactive slots have only 12. `owners`: the owner of a fine brick lies in the same aligned group of 8 space devices as the brick; no two bricks of one device have the same owner, so each owner receives at most one brick from each device. `octslots`: no two fine bricks with the same owner share a value.
All inputs are finite; a program needn't handle non-finite values.
Results may differ from the reference program's by a relative error of at most 0.0075.
Values may be sent and summed in bfloat16 or wider, within the bound.
A program may use at most 128 MiB of HBM per device.

```python
import jax
import jax.numpy as jnp
from jax import lax

FINE_CH = 96
COARSE_CH = 128
BRICKS = 4
SLAB_Y = 4
SLAB_Z = 4
TILES = 8
ALL_BRICKS = 256
COARSE = 2
ALL_COARSE = 128
N_SPACE = 64


def layout_tile(tile_key):
    positions = SLAB_Y * SLAB_Z
    cells = positions // 4
    half_z = SLAB_Z // 2
    devices = jnp.arange(N_SPACE, dtype=jnp.int32)
    cell_orders = jax.vmap(lambda device: jax.random.permutation(jax.random.fold_in(tile_key, 1000 + device), cells))(devices)
    cell_ids = jnp.arange(cells, dtype=jnp.int32)
    child_orders = jax.vmap(lambda device: jax.vmap(lambda cell_one: jax.random.permutation(jax.random.fold_in(jax.random.fold_in(tile_key, 2000 + device), cell_one), 4))(cell_ids))(devices)
    order = jnp.arange(positions, dtype=jnp.int32)
    cell = cell_orders[:, order % cells].astype(jnp.int32)
    child = jnp.take_along_axis(child_orders.reshape(N_SPACE, cells * 4), cell * 4 + order[None, :] // cells, axis=1).astype(jnp.int32)
    place_y = 2 * (cell // half_z) + child // 2
    place_z = 2 * (cell % half_z) + child % 2
    spots = (place_y * SLAB_Z + place_z)[:, :BRICKS].astype(jnp.int32)
    active = jax.random.randint(jax.random.fold_in(tile_key, 7), (N_SPACE,), 5 * BRICKS // 6, BRICKS + 1)
    fullest = jax.random.randint(jax.random.fold_in(tile_key, 8), (), 0, N_SPACE)
    active = jnp.where(devices == fullest, BRICKS, active)
    slots = jnp.arange(BRICKS, dtype=jnp.int32)
    live = slots[None, :] < active[:, None]
    return (spots, live)


def neighbour_tile(tile_key):
    spots, live = layout_tile(tile_key)
    places = jnp.where(live, spots, -1)
    place_y = places // SLAB_Z
    place_z = places % SLAB_Z
    devices = jnp.arange(N_SPACE, dtype=jnp.int32)
    slots = jnp.arange(BRICKS, dtype=jnp.int32)
    columns = []
    for offset in range(27):
        layer_x, layer_y, layer_z = (offset // 9, offset // 3 % 3, offset % 3)
        other = devices + layer_x - 1
        inside = (other >= 0) & (other < N_SPACE)
        target_places = places[jnp.clip(other, 0, N_SPACE - 1)]
        want_y = place_y + layer_y - 1
        want_z = place_z + layer_z - 1
        usable = live & inside[:, None] & (want_y >= 0) & (want_y < SLAB_Y) & (want_z >= 0) & (want_z < SLAB_Z)
        wanted = want_y * SLAB_Z + want_z
        matches = target_places[:, None, :] == wanted[:, :, None]
        found = jnp.any(matches, axis=2)
        which = jnp.sum(matches.astype(jnp.int32) * slots[None, None, :], axis=2)
        columns.append(jnp.where(usable & found, layer_x * BRICKS + which, 3 * BRICKS))
    return jnp.stack(columns, axis=-1).reshape(N_SPACE * BRICKS, 27).astype(jnp.int32)


def occupancy_tile(tile_key):
    spots, live = layout_tile(tile_key)
    levels = jax.random.randint(jax.random.fold_in(tile_key, 5), (N_SPACE, BRICKS, 512), 0, 8)
    return jnp.where(live[:, :, None] & (levels < 5), 1, 0).astype(jnp.int32).reshape(N_SPACE * BRICKS, 512)


def routing_tile(tile_key):
    spots, live = layout_tile(tile_key)
    groups = N_SPACE // 8
    group_ids = jnp.arange(groups, dtype=jnp.int32)
    perms = jax.vmap(lambda group: jax.random.permutation(jax.random.fold_in(tile_key, 600 + group), 8))(group_ids).astype(jnp.int32)
    flips = jax.random.randint(jax.random.fold_in(tile_key, 9), (groups,), 0, 2)
    devices = jnp.arange(N_SPACE, dtype=jnp.int32)[:, None]
    pair_in_group = devices % 8 // 2
    group = devices // 8
    place_y = spots // SLAB_Z
    place_z = spots % SLAB_Z
    cell = place_y // 2 * (SLAB_Z // 2) + place_z // 2
    local_owner = perms[group, 2 * cell + pair_in_group % 2]
    owner_ids = (8 * group + local_owner).astype(jnp.int32)
    coarse_slot = (pair_in_group // 2 + flips[group]) % 2
    octant = 4 * (devices % 2) + 2 * (place_y % 2) + place_z % 2
    slot_ids = (8 * coarse_slot + octant).astype(jnp.int32)
    return (owner_ids.reshape(N_SPACE * BRICKS), slot_ids.reshape(N_SPACE * BRICKS))


def tiles_of(key, salt, maker):
    tiles = jnp.arange(TILES, dtype=jnp.int32)
    return jax.vmap(lambda tile: maker(jax.random.fold_in(jax.random.fold_in(key, salt), tile)))(tiles)


def draw_occupancy(key, part):
    return tiles_of(key, 71, occupancy_tile)


def draw_neighbours(key, part):
    return tiles_of(key, 71, neighbour_tile)


def draw_owners(key, part):
    return tiles_of(key, 71, lambda tile_key: routing_tile(tile_key)[0])


def draw_octslots(key, part):
    return tiles_of(key, 71, lambda tile_key: routing_tile(tile_key)[1])


def block_levels(rng, shape, shards, smallest, top_value):
    gain, own = 1.0, jax.random.fold_in(rng, 6)
    for dim, parts in shards:
        steps = jnp.exp(jax.random.uniform(jax.random.fold_in(own, dim), (parts,), jnp.float32, smallest / len(shards), top_value / len(shards)))
        gain = gain * jnp.repeat(steps, shape[dim] // parts).reshape([-1 if axis == dim else 1 for axis in range(len(shape))])
    return gain


def scatter_about(stream_key, extent, width, bound, cuts=(), held_as=jnp.bfloat16):
    array = width * jax.random.normal(stream_key, extent, jnp.float32)
    if cuts:
        array = array * block_levels(stream_key, extent, cuts, -0.22, 0.18)
    return jnp.clip(array, -bound, bound).astype(held_as)


def setup_inputs(seed: int = 0) -> dict:
    seeds = jax.random.split(jax.random.key(seed), 9)
    return {
        "features": scatter_about(seeds[0], (TILES, ALL_BRICKS, FINE_CH, 512), 1.0, 6.0, ((0, 8), (1, 64))),
        "occupancy": draw_occupancy(jax.random.fold_in(seeds[8], 71), 0),
        "neighbours": draw_neighbours(jax.random.fold_in(seeds[8], 71), 0),
        "owners": draw_owners(jax.random.fold_in(seeds[8], 71), 0),
        "octslots": draw_octslots(jax.random.fold_in(seeds[8], 71), 0),
        "cotangent": scatter_about(seeds[5], (TILES, ALL_COARSE, COARSE_CH, 512), 0.003, 0.046875, ((0, 8), (1, 64))),
        "w_sub": scatter_about(seeds[6], (27, FINE_CH, FINE_CH), (27 * FINE_CH) ** -0.5, 0.125),
        "w_down": scatter_about(seeds[7], (8, COARSE_CH, FINE_CH), (8 * FINE_CH) ** -0.5, 0.21875),
    }


SIDES = ((7, 8), (0, 8), (0, 1))


def assemble(sources, pick_rows):
    slab_parts = []
    for layer_x in range(3):
        row_parts = []
        for layer_y in range(3):
            col_parts = []
            for layer_z in range(3):
                low_y, high_y = SIDES[layer_y]
                low_z, high_z = SIDES[layer_z]
                source_piece = sources[layer_x][:, :, :, low_y:high_y, low_z:high_z]
                col_parts.append(jnp.take(source_piece, pick_rows[layer_x][:, 3 * layer_y + layer_z], axis=0))
            row_parts.append(jnp.concatenate(col_parts, axis=4))
        slab_parts.append(jnp.concatenate(row_parts, axis=3))
    return jnp.concatenate(slab_parts, axis=2)


def octant_pieces(activation):
    bricks, channels = activation.shape[0], activation.shape[1]
    cubes = activation.reshape(bricks, channels, 4, 2, 4, 2, 4, 2)
    result = []
    for octant in range(8):
        result.append(cubes[:, :, :, octant // 4, :, octant // 2 % 2, :, octant % 2].reshape(bricks, channels, 64))
    return result


def spread(pieces):
    bricks, channels = pieces[0].shape[0], pieces[0].shape[1]
    stacked = jnp.stack(pieces).reshape(2, 2, 2, bricks, channels, 4, 4, 4)
    return jnp.transpose(stacked, (3, 4, 5, 0, 6, 1, 7, 2)).reshape(bricks, channels, 512)


def to_coarse(octant_table):
    slots = octant_table.shape[0] // 8
    chans = octant_table.shape[1]
    shaped = octant_table.reshape(slots, 2, 2, 2, chans, 4, 4, 4)
    return jnp.transpose(shaped, (0, 4, 1, 5, 2, 6, 3, 7)).reshape(slots, chans, 512)


def from_coarse(cubes):
    slots, chans = cubes.shape[0], cubes.shape[1]
    shaped = cubes.reshape(slots, chans, 2, 4, 2, 4, 2, 4)
    return jnp.transpose(shaped, (0, 2, 4, 6, 1, 3, 5, 7)).reshape(slots * 8, chans, 64)


def one_tile(inputs, w_sub, w_down):
    feats, occupied, neighbour_ids, owner_ids, slot_ids, cotangent_tile = inputs
    total_bricks = feats.shape[0]
    channels = feats.shape[1]
    occ_bf = occupied.astype(jnp.bfloat16)
    masked = (feats * occ_bf[:, None, :]).astype(jnp.bfloat16)
    blocks = masked.reshape(total_bricks, channels, 8, 8, 8)
    empty = jnp.zeros((1, channels, 8, 8, 8), jnp.bfloat16)
    sources = (jnp.concatenate([blocks[:, :, 7:8], empty[:, :, 0:1]], axis=0),
               jnp.concatenate([blocks, empty], axis=0),
               jnp.concatenate([blocks[:, :, 0:1], empty[:, :, 0:1]], axis=0))
    device_of = jnp.arange(total_bricks, dtype=jnp.int32) // BRICKS
    pick_rows = []
    for layer_x in range(3):
        column = neighbour_ids[:, 9 * layer_x:9 * layer_x + 9].astype(jnp.int32)
        global_ids = (device_of[:, None] + layer_x - 1) * BRICKS + column - layer_x * BRICKS
        pick_rows.append(jnp.where(column == 3 * BRICKS, total_bricks, global_ids).astype(jnp.int32))
    window = assemble(sources, pick_rows)
    window_f = window.astype(jnp.float32)
    w_sub_f = w_sub.astype(jnp.float32)
    summed = jnp.zeros((total_bricks, channels, 512), jnp.float32)
    for offset in range(27):
        shift_x, shift_y, shift_z = offset // 9, offset // 3 % 3, offset % 3
        window_view = window_f[:, :, shift_x:shift_x + 8, shift_y:shift_y + 8, shift_z:shift_z + 8].reshape(total_bricks, channels, 512)
        summed = summed + jnp.einsum("oc,bcv->bov", w_sub_f[offset], window_view)
    pre_act = summed * occupied.astype(jnp.float32)[:, None, :]
    activation = jnp.maximum(pre_act, 0.0).astype(jnp.bfloat16)
    pieces = [piece_one.astype(jnp.float32) for piece_one in octant_pieces(activation)]
    w_down_f = w_down.astype(jnp.float32)
    octant_sum = jnp.zeros((total_bricks, w_down.shape[1], 64), jnp.float32)
    for octant in range(8):
        octant_sum = octant_sum + jnp.einsum("oc,bcv->bov", w_down_f[octant], pieces[octant])
    octant_out = octant_sum.astype(jnp.bfloat16)
    target = (owner_ids * (COARSE * 8) + slot_ids).astype(jnp.int32)
    octant_table = jnp.zeros((total_bricks // BRICKS * COARSE * 8, w_down.shape[1], 64), jnp.bfloat16)
    octant_table = octant_table.at[target].set(octant_out)
    coarse_tile = to_coarse(octant_table)
    returned = jnp.take(from_coarse(cotangent_tile), target, axis=0)
    returned_f = returned.astype(jnp.float32)
    grad_down_tile = jnp.stack([jnp.einsum("bov,bcv->oc", returned_f, pieces[octant]) for octant in range(8)])
    grad_pieces = [jnp.einsum("oc,bov->bcv", w_down_f[octant], returned_f) for octant in range(8)]
    grad_act = spread(grad_pieces)
    grad_pre = jnp.where(pre_act > 0, grad_act, 0.0).astype(jnp.bfloat16).astype(jnp.float32)
    grad_list = []
    for offset in range(27):
        shift_x, shift_y, shift_z = offset // 9, offset // 3 % 3, offset % 3
        window_view = window_f[:, :, shift_x:shift_x + 8, shift_y:shift_y + 8, shift_z:shift_z + 8].reshape(total_bricks, channels, 512)
        grad_list.append(jnp.einsum("bov,bcv->oc", grad_pre, window_view))
    grad_sub_tile = jnp.stack(grad_list)
    return coarse_tile, grad_sub_tile, grad_down_tile


def reference(features, occupancy, neighbours, owners, octslots, cotangent, w_sub, w_down):
    def runner(inputs):
        return one_tile(inputs, w_sub, w_down)

    coarse, grad_subs, grad_downs = lax.map(runner, (features, occupancy, neighbours, owners, octslots, cotangent))
    return coarse, jnp.sum(grad_subs, axis=0), jnp.sum(grad_downs, axis=0)
```

```python
import functools

import jax
import jax.numpy as jnp
from jax import lax
from jax.experimental import pallas as pl
from jax.experimental.pallas import tpu as pltpu
from jax.sharding import PartitionSpec as P

SIDES = ((7, 8), (0, 8), (0, 1))


def boundary_planes(masked):
    bricks, channels = masked.shape[:2]
    ends = lax.axis_size("space") - 1
    up = [(i, i + 1) for i in range(ends)]
    down = [(i + 1, i) for i in range(ends)]
    lower = lax.ppermute(masked[:, :, 448:], "space", up)
    upper = lax.ppermute(masked[:, :, :64], "space", down)
    shape = (bricks, channels, 1, 8, 8)
    return lower.reshape(shape), upper.reshape(shape)


def as_sent(shard):
    return jax.tree.map(lambda a: a.astype(jnp.bfloat16) if a.dtype == jnp.float32 else a, shard)


def swapped(block, axis, distance):
    count = lax.axis_size(axis)
    route = []
    for low in range(count):
        high = low | 1 << distance
        if high != low and high < count:
            route += [(low, high), (high, low)]
    return lax.ppermute(block, axis, route)


def assemble(sources, pick_rows):
    slab_parts = []
    for layer_x in range(3):
        row_parts = []
        for layer_y in range(3):
            col_parts = []
            for layer_z in range(3):
                low_y, high_y = SIDES[layer_y]
                low_z, high_z = SIDES[layer_z]
                source_piece = sources[layer_x][:, :, :, low_y:high_y, low_z:high_z]
                col_parts.append(
                    jnp.take(source_piece, pick_rows[layer_x][:, 3 * layer_y + layer_z], axis=0)
                )
            row_parts.append(jnp.concatenate(col_parts, axis=4))
        slab_parts.append(jnp.concatenate(row_parts, axis=3))
    return jnp.concatenate(slab_parts, axis=2)


def octant_pieces(activation):
    bricks, channels = (activation.shape[0], activation.shape[1])
    cubes = activation.reshape(bricks, channels, 4, 2, 4, 2, 4, 2)
    result = []
    for octant in range(8):
        result.append(
            cubes[:, :, :, octant // 4, :, octant // 2 % 2, :, octant % 2].reshape(
                bricks, channels, 64
            )
        )
    return result


def spread(pieces):
    bricks, channels = (pieces[0].shape[0], pieces[0].shape[1])
    stacked = jnp.stack(pieces).reshape(2, 2, 2, bricks, channels, 4, 4, 4)
    return jnp.transpose(stacked, (3, 4, 5, 0, 6, 1, 7, 2)).reshape(bricks, channels, 512)


def to_coarse(octant_table):
    slots = octant_table.shape[0] // 8
    chans = octant_table.shape[1]
    shaped = octant_table.reshape(slots, 2, 2, 2, chans, 4, 4, 4)
    return jnp.transpose(shaped, (0, 4, 1, 5, 2, 6, 3, 7)).reshape(slots, chans, 512)


def from_coarse(cubes):
    slots, chans = (cubes.shape[0], cubes.shape[1])
    shaped = cubes.reshape(slots, chans, 2, 4, 2, 4, 2, 4)
    return jnp.transpose(shaped, (0, 2, 4, 6, 1, 3, 5, 7)).reshape(slots * 8, chans, 64)


def row_views(window, row_index):
    shift_x, shift_y = (row_index // 3, row_index % 3)
    bricks, channels = (window.shape[0], window.shape[1])
    views = []
    for shift_z in range(3):
        views.append(
            window[
                :, :, shift_x : shift_x + 8, shift_y : shift_y + 8, shift_z : shift_z + 8
            ].reshape(bricks, channels, 512)
        )
    return jnp.concatenate(views, axis=1)


def row_kernel(w_sub, row_index):
    part_w = w_sub[3 * row_index : 3 * row_index + 3]
    outs, chans = (part_w.shape[1], part_w.shape[2])
    return jnp.transpose(part_w, (1, 0, 2)).reshape(outs, 3 * chans)


def group_route(parts, position, sender):
    current = parts
    for bit in range(3):
        flag = position // (1 << bit) % 2 == 1
        sends, keeps = ([], [])
        for member in current:
            shaped = member.reshape((8 >> bit + 1, 2, 1 << bit) + member.shape[1:])
            low_half = shaped[:, 0]
            high_half = shaped[:, 1]
            sends.append(jnp.where(flag, low_half, high_half))
            keeps.append(jnp.where(flag, high_half, low_half))
        arrived = sender(tuple(sends), bit)
        updated = []
        for member, kept, got in zip(current, keeps, arrived):
            new_low = jnp.where(flag, got, kept)
            new_high = jnp.where(flag, kept, got)
            updated.append(jnp.stack([new_low, new_high], axis=1).reshape(member.shape))
        current = tuple(updated)
    return current


MESH = pl.DeviceIdType.MESH
NY = 8
PIECE = 48
QUARTER = NY * PIECE


class Place:
    def __init__(self, sizes):
        self.nz, self.nx = sizes
        space, rep = lax.axis_index("space"), lax.axis_index("rep")
        self.z, self.y = space // NY, space % NY
        self.x, self.core = rep // 2, rep % 2

    def across(self):
        return (self.z * NY + self.y, self.x * 2 + 1 - self.core)

    def along_x(self, k):
        return (self.z * NY + self.y, (self.x + k) % self.nx * 2 + self.core)

    def along_y(self, k):
        return (self.z * NY + (self.y + k) % NY, self.x * 2 + self.core)

    def along_z(self, k):
        return ((self.z + k) % self.nz * NY + self.y, self.x * 2 + self.core)

    def sum_partners(self):
        near = [self.across()]
        near += [self.along_x(k) for k in range(1, self.nx)]
        near += [self.along_y(k) for k in range(1, NY)]
        near += [self.along_z(k) for k in range(1, self.nz)]
        return near


def greet(partners):
    barrier = pltpu.get_barrier_semaphore()
    for partner in partners:
        pl.semaphore_signal(barrier, inc=1, device_id=partner, device_id_type=MESH)
    pl.semaphore_wait(barrier, len(partners))


def rows_at(start, count):
    return pl.ds(pl.multiple_of(start, 16), count)


def sum_scratch(sizes):
    nz, nx = sizes
    half = nx * QUARTER
    copies = 2 * nx + 2 * (nx - 1) + 2 * (NY - 1) + (nz - 1)
    return [
        pltpu.VMEM((half, 128), jnp.bfloat16),
        pltpu.VMEM((half, 128), jnp.bfloat16),
        pltpu.VMEM((nx - 1, QUARTER, 128), jnp.bfloat16),
        pltpu.VMEM((nx - 1, QUARTER, 128), jnp.bfloat16),
        pltpu.VMEM((QUARTER, 128), jnp.float32),
        pltpu.VMEM((QUARTER, 128), jnp.bfloat16),
        pltpu.VMEM((NY - 1, PIECE, 128), jnp.bfloat16),
        pltpu.VMEM((nz, PIECE, 128), jnp.bfloat16),
        pltpu.VMEM((2 * half, 128), jnp.bfloat16),
        pltpu.SemaphoreType.DMA((copies,)),
        pltpu.SemaphoreType.DMA((copies,)),
    ]


class GradSum:
    def __init__(self, place, scratch):
        self.place = place
        (self.core_out, self.core_in, self.x_out, self.x_in, self.mine, self.y_out,
         self.y_in, self.z_all, self.total, self.send_sem, self.recv_sem) = scratch
        self.used = 0
        self.sent = []

    def slot(self):
        self.used += 1
        return self.used - 1

    def send(self, slot, src, dst, device):
        copy = pltpu.make_async_remote_copy(
            src_ref=src, dst_ref=dst, send_sem=self.send_sem.at[slot],
            recv_sem=self.recv_sem.at[slot], device_id=device, device_id_type=MESH)
        copy.start()
        self.sent.append(copy)

    def arrive(self, slot, dst, device):
        pltpu.make_async_remote_copy(
            src_ref=dst, dst_ref=dst, send_sem=self.send_sem.at[slot],
            recv_sem=self.recv_sem.at[slot], device_id=device, device_id_type=MESH).wait_recv()

    def run(self, grads):
        at = self.place
        nx, nz = at.nx, at.nz
        half = nx * QUARTER
        x, y, z, core = at.x, at.y, at.z, at.core
        f32, bf16 = jnp.float32, jnp.bfloat16

        def quarter(i):
            return rows_at((x + 1 + i) % nx * QUARTER, QUARTER)

        core_slots = [self.slot() for _ in range(nx)]
        for i in range(nx):
            start = (1 - core) * half + (x + 1 + i) % nx * QUARTER
            self.core_out[quarter(i)] = grads[rows_at(start, QUARTER)].astype(bf16)
            self.send(core_slots[i], self.core_out.at[quarter(i)], self.core_in.at[quarter(i)],
                      at.across())
        x_slots = [self.slot() for _ in range(nx - 1)]
        for i in range(nx):
            self.arrive(core_slots[i], self.core_in.at[quarter(i)], at.across())
            start = core * half + (x + 1 + i) % nx * QUARTER
            pair = grads[rows_at(start, QUARTER)] + self.core_in[quarter(i)].astype(f32)
            if i < nx - 1:
                self.x_out[i] = pair.astype(bf16)
                self.send(x_slots[i], self.x_out.at[i], self.x_in.at[i], at.along_x(i + 1))
            else:
                self.mine[...] = pair
        for i in range(nx - 1):
            self.arrive(x_slots[i], self.x_in.at[i], at.along_x(-i - 1))
            self.mine[...] += self.x_in[i].astype(f32)
        self.y_out[...] = self.mine[...].astype(bf16)
        y_slots = [self.slot() for _ in range(NY - 1)]
        for k in range(1, NY):
            self.send(y_slots[k - 1], self.y_out.at[rows_at((y + k) % NY * PIECE, PIECE)],
                      self.y_in.at[k - 1], at.along_y(k))
        piece = self.mine[rows_at(y * PIECE, PIECE)]
        for k in range(1, NY):
            self.arrive(y_slots[k - 1], self.y_in.at[k - 1], at.along_y(-k))
            piece = piece + self.y_in[k - 1].astype(f32)
        self.z_all[z] = piece.astype(bf16)
        z_slots = [self.slot() for _ in range(nz - 1)]
        for k in range(1, nz):
            self.send(z_slots[k - 1], self.z_all.at[z], self.z_all.at[z], at.along_z(k))
        for k in range(1, nz):
            self.arrive(z_slots[k - 1], self.z_all.at[(z - k) % nz], at.along_z(-k))
        piece = self.z_all[0].astype(f32)
        for layer in range(1, nz):
            piece = piece + self.z_all[layer].astype(f32)
        base = core * half + x * QUARTER

        def piece_rows(k):
            return rows_at(base + (y + k) % NY * PIECE, PIECE)

        self.total[piece_rows(0)] = piece.astype(bf16)
        y_slots = [self.slot() for _ in range(NY - 1)]
        for k in range(1, NY):
            self.send(y_slots[k - 1], self.total.at[piece_rows(0)], self.total.at[piece_rows(0)],
                      at.along_y(k))
        for k in range(1, NY):
            self.arrive(y_slots[k - 1], self.total.at[piece_rows(-k)], at.along_y(-k))

        def quarter_of(which, k):
            return rows_at(which * half + (x + k) % nx * QUARTER, QUARTER)

        x_slots = [self.slot() for _ in range(nx - 1)]
        core_slots = [self.slot() for _ in range(nx)]
        own = self.total.at[quarter_of(core, 0)]
        for k in range(1, nx):
            self.send(x_slots[k - 1], own, own, at.along_x(k))
        self.send(core_slots[0], own, own, at.across())
        for k in range(1, nx):
            other = self.total.at[quarter_of(core, -k)]
            self.arrive(x_slots[k - 1], other, at.along_x(-k))
            self.send(core_slots[k], other, other, at.across())
        for k in range(nx):
            self.arrive(core_slots[k], self.total.at[quarter_of(1 - core, -k)], at.across())

    def finish(self):
        for copy in self.sent:
            copy.wait_send()


def sum_kernel(sizes, grads_ref, out_ref, *scratch):
    place = Place(sizes)
    greet(place.sum_partners())
    work = GradSum(place, scratch)
    work.run(grads_ref)
    out_ref[...] = work.total[...].astype(jnp.float32)
    work.finish()


def summed_over_all(sizes, grads):
    return pl.pallas_call(
        functools.partial(sum_kernel, sizes),
        out_shape=jax.ShapeDtypeStruct(grads.shape, jnp.float32),
        in_specs=[pl.BlockSpec(memory_space=pltpu.VMEM)],
        out_specs=pl.BlockSpec(memory_space=pltpu.VMEM),
        scratch_shapes=sum_scratch(sizes),
        compiler_params=pltpu.CompilerParams(
            collective_id=0, has_side_effects=True, vmem_limit_bytes=48 * 2**20
        ),
    )(grads)


def per_device(sizes, features, occupancy, neighbours, owners, octslots, cotangent, w_sub, w_down):
    occupied = occupancy[0]
    masked = features[0] * occupied.astype(jnp.bfloat16)[:, None, :]
    bricks, channels = (masked.shape[0], masked.shape[1])
    out_chans = w_down.shape[1]
    blocks = masked.reshape(bricks, channels, 8, 8, 8)
    lower_plane, upper_plane = boundary_planes(masked)
    empty_plane = jnp.zeros((1, channels, 1, 8, 8), jnp.bfloat16)
    empty_block = jnp.zeros((1, channels, 8, 8, 8), jnp.bfloat16)
    sources = (
        jnp.concatenate([lower_plane, empty_plane], axis=0),
        jnp.concatenate([blocks, empty_block], axis=0),
        jnp.concatenate([upper_plane, empty_plane], axis=0),
    )
    neighbour_ids = neighbours[0]
    pick_rows = []
    for layer_x in range(3):
        column = neighbour_ids[:, 9 * layer_x : 9 * layer_x + 9]
        pick_rows.append(jnp.where(column == 3 * bricks, bricks, column - layer_x * bricks))
    window = assemble(sources, pick_rows)
    summed = jnp.zeros((bricks, channels, 512), jnp.float32)
    for row_index in range(9):
        summed = summed + jnp.einsum(
            "ok,bkv->bov",
            row_kernel(w_sub, row_index),
            row_views(window, row_index),
            preferred_element_type=jnp.float32,
        )
    pre_act = summed * occupied.astype(jnp.float32)[:, None, :]
    activation = jnp.maximum(pre_act, 0.0).astype(jnp.bfloat16)
    pieces = octant_pieces(activation)
    octant_sum = jnp.zeros((bricks, out_chans, 64), jnp.float32)
    for octant in range(8):
        octant_sum = octant_sum + jnp.einsum(
            "oc,bcv->bov", w_down[octant], pieces[octant], preferred_element_type=jnp.float32
        )
    octant_flat = octant_sum.astype(jnp.bfloat16).reshape(bricks, out_chans * 64)
    capacity = (bricks + 3) // 4
    position = lax.axis_index("space")
    local_owner = owners[0] % 8
    slot_ids = octslots[0]
    brick_order = jnp.arange(bricks, dtype=jnp.int32)
    same_owner = local_owner[:, None] == local_owner[None, :]
    send_rank = jnp.sum(
        (same_owner & (brick_order[None, :] < brick_order[:, None])).astype(jnp.int32), axis=1
    )
    routing = (local_owner[None, None, :] == jnp.arange(8, dtype=jnp.int32)[:, None, None]) & (
        send_rank[None, None, :] == jnp.arange(capacity, dtype=jnp.int32)[None, :, None]
    )
    routing_bf = routing.astype(jnp.bfloat16)
    outgoing = jnp.einsum(
        "dmj,jf->dmf", routing_bf, octant_flat, preferred_element_type=jnp.float32
    ).astype(jnp.bfloat16)
    labels = jnp.sum(routing.astype(jnp.int32) * (slot_ids + 1)[None, None, :], axis=2) - 1

    def send_octants(parts, bit):
        return jax.tree.map(
            lambda part, own: part.astype(own.dtype), swapped(as_sent(parts), "space", bit), parts
        )

    incoming, incoming_labels = group_route((outgoing, labels), position, send_octants)
    arrivals = 8 * capacity
    octant_slots = cotangent.shape[1] * 8
    placing = (
        incoming_labels.reshape(arrivals)[None, :]
        == jnp.arange(octant_slots, dtype=jnp.int32)[:, None]
    ).astype(jnp.bfloat16)
    coarse_table = jnp.einsum(
        "on,nf->of",
        placing,
        incoming.reshape(arrivals, out_chans * 64),
        preferred_element_type=jnp.float32,
    ).astype(jnp.bfloat16)
    coarse = to_coarse(coarse_table.reshape(octant_slots, out_chans, 64))[None]
    cot_table = from_coarse(cotangent[0]).reshape(octant_slots, out_chans * 64)
    answers = jnp.einsum(
        "on,of->nf", placing, cot_table, preferred_element_type=jnp.float32
    ).astype(jnp.bfloat16)

    def send_returns(parts, bit):
        return jax.tree.map(
            lambda part, own: part.astype(own.dtype), swapped(as_sent(parts), "space", bit), parts
        )

    replies = group_route((answers.reshape(8, capacity, out_chans * 64),), position, send_returns)[
        0
    ]
    returned = (
        jnp.einsum("dmj,dmf->jf", routing_bf, replies, preferred_element_type=jnp.float32)
        .astype(jnp.bfloat16)
        .reshape(bricks, out_chans, 64)
    )
    grad_down_local = jnp.stack(
        [
            jnp.einsum("bov,bcv->oc", returned, pieces[octant], preferred_element_type=jnp.float32)
            for octant in range(8)
        ]
    )
    grad_pieces = [
        jnp.einsum("oc,bov->bcv", w_down[octant], returned, preferred_element_type=jnp.float32)
        for octant in range(8)
    ]
    grad_act = spread(grad_pieces)
    grad_pre = jnp.where(pre_act > 0, grad_act, 0.0).astype(jnp.bfloat16)
    grad_list = []
    for row_index in range(9):
        row_grad = jnp.einsum(
            "bov,bkv->ok",
            grad_pre,
            row_views(window, row_index),
            preferred_element_type=jnp.float32,
        )
        grad_list.append(jnp.transpose(row_grad.reshape(channels, 3, channels), (1, 0, 2)))
    grad_sub_local = jnp.concatenate(grad_list, axis=0)
    flat = jnp.concatenate([grad_sub_local.reshape(-1), grad_down_local.reshape(-1)])
    rows = 2 * sizes[1] * QUARTER
    flat = jnp.pad(flat, (0, rows * 128 - flat.shape[0]))
    flat = summed_over_all(sizes, flat.reshape(rows, 128)).reshape(-1)
    count = grad_sub_local.size
    grad_sub = flat[:count].reshape(grad_sub_local.shape)
    grad_down = flat[count : count + grad_down_local.size].reshape(grad_down_local.shape)
    return (coarse, grad_sub, grad_down)


def solution(mesh):
    sizes = (mesh.shape["space"] // NY, mesh.shape["rep"] // 2)
    return jax.shard_map(
        functools.partial(per_device, sizes),
        mesh=mesh,
        in_specs=(
            P("rep", "space", None, None),
            P("rep", "space", None),
            P("rep", "space", None),
            P("rep", "space"),
            P("rep", "space"),
            P("rep", "space", None, None),
            P(),
            P(),
        ),
        out_specs=(P("rep", "space", None, None), P(), P()),
        check_vma=False,
    )
```

```python
import functools

import jax
import jax.numpy as jnp
import numpy as np
from jax import lax
from jax.experimental import pallas as pl
from jax.experimental.pallas import tpu as pltpu
from jax.sharding import PartitionSpec as P

MESH = pl.DeviceIdType.MESH
NY = 8
PIECE = 48
QUARTER = NY * PIECE


class Place:
    def __init__(self, sizes):
        self.nz, self.nx = sizes
        space, rep = lax.axis_index("space"), lax.axis_index("rep")
        self.z, self.y = space // NY, space % NY
        self.x, self.core = rep // 2, rep % 2

    def across(self):
        return (self.z * NY + self.y, self.x * 2 + 1 - self.core)

    def along_x(self, k):
        return (self.z * NY + self.y, (self.x + k) % self.nx * 2 + self.core)

    def along_y(self, k):
        return (self.z * NY + (self.y + k) % NY, self.x * 2 + self.core)

    def along_z(self, k):
        return ((self.z + k) % self.nz * NY + self.y, self.x * 2 + self.core)

    def sum_partners(self):
        near = [self.across()]
        near += [self.along_x(k) for k in range(1, self.nx)]
        near += [self.along_y(k) for k in range(1, NY)]
        near += [self.along_z(k) for k in range(1, self.nz)]
        return near


def rows_at(start, count):
    return pl.ds(pl.multiple_of(start, 16), count)


def sum_scratch(sizes):
    nz, nx = sizes
    half = nx * QUARTER
    copies = 2 * nx + 2 * (nx - 1) + 2 * (NY - 1) + (nz - 1)
    return [
        pltpu.VMEM((half, 128), jnp.bfloat16),
        pltpu.VMEM((half, 128), jnp.bfloat16),
        pltpu.VMEM((nx - 1, QUARTER, 128), jnp.bfloat16),
        pltpu.VMEM((nx - 1, QUARTER, 128), jnp.bfloat16),
        pltpu.VMEM((QUARTER, 128), jnp.float32),
        pltpu.VMEM((QUARTER, 128), jnp.bfloat16),
        pltpu.VMEM((NY - 1, PIECE, 128), jnp.bfloat16),
        pltpu.VMEM((nz, PIECE, 128), jnp.bfloat16),
        pltpu.VMEM((2 * half, 128), jnp.bfloat16),
        pltpu.SemaphoreType.DMA((copies,)),
        pltpu.SemaphoreType.DMA((copies,)),
    ]


class GradSum:
    def __init__(self, place, scratch):
        self.place = place
        (self.core_out, self.core_in, self.x_out, self.x_in, self.mine, self.y_out,
         self.y_in, self.z_all, self.total, self.send_sem, self.recv_sem) = scratch
        self.used = 0
        self.sent = []

    def slot(self):
        self.used += 1
        return self.used - 1

    def send(self, slot, src, dst, device):
        copy = pltpu.make_async_remote_copy(
            src_ref=src, dst_ref=dst, send_sem=self.send_sem.at[slot],
            recv_sem=self.recv_sem.at[slot], device_id=device, device_id_type=MESH)
        copy.start()
        self.sent.append(copy)

    def arrive(self, slot, dst, device):
        pltpu.make_async_remote_copy(
            src_ref=dst, dst_ref=dst, send_sem=self.send_sem.at[slot],
            recv_sem=self.recv_sem.at[slot], device_id=device, device_id_type=MESH).wait_recv()

    def run(self, grads, meanwhile):
        at = self.place
        nx, nz = at.nx, at.nz
        half = nx * QUARTER
        x, y, z, core = at.x, at.y, at.z, at.core

        def quarter(i):
            return rows_at((x + 1 + i) % nx * QUARTER, QUARTER)

        core_slots = [self.slot() for _ in range(nx)]
        for i in range(nx):
            start = (1 - core) * half + (x + 1 + i) % nx * QUARTER
            self.core_out[quarter(i)] = grads[rows_at(start, QUARTER)].astype(BF16)
            self.send(core_slots[i], self.core_out.at[quarter(i)], self.core_in.at[quarter(i)],
                      at.across())
        x_slots = [self.slot() for _ in range(nx - 1)]
        for i in range(nx):
            self.arrive(core_slots[i], self.core_in.at[quarter(i)], at.across())
            start = core * half + (x + 1 + i) % nx * QUARTER
            pair = grads[rows_at(start, QUARTER)] + self.core_in[quarter(i)].astype(F32)
            if i < nx - 1:
                self.x_out[i] = pair.astype(BF16)
                self.send(x_slots[i], self.x_out.at[i], self.x_in.at[i], at.along_x(i + 1))
            else:
                self.mine[...] = pair
        for i in range(nx - 1):
            self.arrive(x_slots[i], self.x_in.at[i], at.along_x(-i - 1))
            self.mine[...] += self.x_in[i].astype(F32)
        self.y_out[...] = self.mine[...].astype(BF16)
        y_slots = [self.slot() for _ in range(NY - 1)]
        for k in range(1, NY):
            self.send(y_slots[k - 1], self.y_out.at[rows_at((y + k) % NY * PIECE, PIECE)],
                      self.y_in.at[k - 1], at.along_y(k))
        meanwhile()
        piece = self.mine[rows_at(y * PIECE, PIECE)]
        for k in range(1, NY):
            self.arrive(y_slots[k - 1], self.y_in.at[k - 1], at.along_y(-k))
            piece = piece + self.y_in[k - 1].astype(F32)
        self.z_all[z] = piece.astype(BF16)
        z_slots = [self.slot() for _ in range(nz - 1)]
        for k in range(1, nz):
            self.send(z_slots[k - 1], self.z_all.at[z], self.z_all.at[z], at.along_z(k))
        for k in range(1, nz):
            self.arrive(z_slots[k - 1], self.z_all.at[(z - k) % nz], at.along_z(-k))
        piece = self.z_all[0].astype(F32)
        for layer in range(1, nz):
            piece = piece + self.z_all[layer].astype(F32)
        base = core * half + x * QUARTER

        def piece_rows(k):
            return rows_at(base + (y + k) % NY * PIECE, PIECE)

        self.total[piece_rows(0)] = piece.astype(BF16)
        y_slots = [self.slot() for _ in range(NY - 1)]
        for k in range(1, NY):
            self.send(y_slots[k - 1], self.total.at[piece_rows(0)], self.total.at[piece_rows(0)],
                      at.along_y(k))
        for k in range(1, NY):
            self.arrive(y_slots[k - 1], self.total.at[piece_rows(-k)], at.along_y(-k))

        def quarter_of(which, k):
            return rows_at(which * half + (x + k) % nx * QUARTER, QUARTER)

        x_slots = [self.slot() for _ in range(nx - 1)]
        core_slots = [self.slot() for _ in range(nx)]
        own = self.total.at[quarter_of(core, 0)]
        for k in range(1, nx):
            self.send(x_slots[k - 1], own, own, at.along_x(k))
        self.send(core_slots[0], own, own, at.across())
        for k in range(1, nx):
            other = self.total.at[quarter_of(core, -k)]
            self.arrive(x_slots[k - 1], other, at.along_x(-k))
            self.send(core_slots[k], other, other, at.across())
        for k in range(nx):
            self.arrive(core_slots[k], self.total.at[quarter_of(1 - core, -k)], at.across())

    def finish(self):
        for copy in self.sent:
            copy.wait_send()

F32, BF16 = jnp.float32, jnp.bfloat16
NT = (((1,), (1,)), ((), ()))
NN = (((1,), (0,)), ((), ()))
TN = (((0,), (0,)), ((), ()))
BRICKS = 4
FINE = 96
COARSE = 128
TAPS = 9
SUB_ROWS = 3 * FINE
SUB_BLOCKS = 7
DOWN_ROWS = 2 * COARSE
DOWN_START = SUB_ROWS * SUB_BLOCKS
USED_ROWS = DOWN_START + 3 * DOWN_ROWS


def mul(a, b, dims=NN):
    return lax.dot_general(a, b, dims, preferred_element_type=F32)


def padding_matrix():
    out = np.zeros((9, 2, 8, 8, 2, 128), np.float32)
    sides = ([(7, 0)], [(i, i + 1) for i in range(8)], [(0, 9)])
    for layer_y in range(3):
        for layer_z in range(3):
            for y, to_y in sides[layer_y]:
                for z, to_z in sides[layer_z]:
                    for half in range(2):
                        out[3 * layer_y + layer_z, half, y, z, half, 10 * to_y + to_z] = 1
    return out.reshape(9 * 128, 256).astype(jnp.bfloat16)


def octant_matrix():
    out = np.zeros((8, 128, 8, 64), np.float32)
    for x in range(8):
        for y in range(8):
            for z in range(8):
                octant = x % 2 * 4 + y % 2 * 2 + z % 2
                out[x, 10 * (y + 1) + z + 1, octant, x // 2 * 16 + y // 2 * 4 + z // 2] = 1
    return out.reshape(1024, 512).astype(jnp.bfloat16)


def placing_matrix():
    out = np.zeros((8, 2, 64, 8, 8, 8), np.float32)
    for octant in range(8):
        for v in range(64):
            x, y, z = v // 16, v // 4 % 4, v % 4
            spot = (octant // 4 * 4 + x, octant // 2 % 2 * 4 + y, octant % 2 * 4 + z)
            out[(octant, slice(None), v) + spot] = 1
    return out.reshape(1024, 512).astype(jnp.bfloat16)


def low_lanes(shape):
    return lax.broadcasted_iota(jnp.int32, shape, len(shape) - 1) % 128 < 64


def packed(block):
    return jnp.where(low_lanes((64, 128)), block[:64], block[64:])


def chosen(labels, slot, table):
    hit = jnp.where(labels[0:1] == slot, 1.0, 0.0).astype(BF16)
    return hit * table


def kernel(sizes, neighbours, owners, octslots, features, occupancy, cotangent, w_sub, w_down,
           pad_m, oct_m, place_m, coarse, grad_sub, grad_down,
           source, upper, lower, gathered, edge, window, wide, occ_pad, active, act_oct, w_cat, w_pair,
           oct_pack, oct_out, oct_in, lab_out, lab_in, table, rep_out, rep_in, returned, ret_half,
           back, shifted, grads, place_in, pair_send, pair_recv, *sum_refs):
    at = Place(sizes)
    work = GradSum(at, sum_refs)
    nspace = at.nz * NY
    me = at.z * NY + at.y
    rep = at.x * 2 + at.core
    above, below = ((me + 1) % nspace, rep), ((me + nspace - 1) % nspace, rep)
    partners = at.sum_partners() + [above, below]
    barrier = pltpu.get_barrier_semaphore()
    for partner in partners:
        pl.semaphore_signal(barrier, inc=1, device_id=partner, device_id_type=MESH)

    def link(slot, src, dst, device):
        return pltpu.make_async_remote_copy(
            src_ref=src, dst_ref=dst, send_sem=pair_send.at[slot], recv_sem=pair_recv.at[slot],
            device_id=device, device_id_type=MESH)

    started = []

    def send(slot, src, dst, device):
        copy = link(slot, src, dst, device)
        copy.start()
        started.append(copy)

    occ = occupancy[...].astype(BF16)
    for j in range(BRICKS):
        source[j] = features[j] * occ[j:j + 1]
    source[BRICKS] = jnp.zeros((FINE, 512), BF16)
    upper[BRICKS] = jnp.zeros((FINE, 128), BF16)
    lower[BRICKS] = jnp.zeros((FINE, 128), BF16)
    owner_of = [owners[j] % NY for j in range(BRICKS)]

    def brick_for(member):
        found = BRICKS
        for j in range(BRICKS):
            found = jnp.where(owner_of[j] == member, j, found)
        return found

    for k in range(NY):
        member = (at.y + k) % NY
        label = -1
        for j in range(BRICKS):
            label = jnp.where(owner_of[j] == member, octslots[j], label)
        lab_out[k] = jnp.full((8, 128), label, jnp.int32)

    pl.semaphore_wait(barrier, len(partners))
    first, last = pl.ds(0, BRICKS), pl.ds(384, 128)
    send(0, source.at[first, :, last], lower.at[first], above)
    send(1, source.at[first, :, pl.ds(0, 128)], upper.at[first], below)
    for k in range(1, NY):
        send(1 + k, lab_out.at[k], lab_in.at[k], at.along_y(k))
    lab_in[0] = lab_out[0]

    spread = mul(cotangent[...].reshape(2 * COARSE, 512), place_m[...], NT)
    for s in range(2):
        for m in range(8):
            block = spread[s * COARSE:(s + 1) * COARSE, m * 128:(m + 1) * 128]
            table[8 * s + m] = packed(block).astype(BF16)
    for kx in range(3):
        w_cat[kx * FINE:(kx + 1) * FINE] = jnp.concatenate(
            [w_sub[TAPS * kx + t] for t in range(TAPS)], axis=1)
    for parity in range(2):
        w_pair[parity * COARSE:(parity + 1) * COARSE] = jnp.concatenate(
            [w_down[2 * pair + parity] for pair in range(4)], axis=1)
    center = pad_m[pl.ds(4 * 128, 128)]
    for p in range(4):
        occ_pad[:, p * 256:(p + 1) * 256] = mul(occ[:, p * 128:(p + 1) * 128], center)

    for k in range(NY):
        if k:
            link(1 + k, lab_out.at[k], lab_in.at[k], at.along_y(-k)).wait_recv()
        labels = lab_in[k]
        answer = chosen(labels, 0, table[0])
        for slot in range(1, 16):
            answer = answer + chosen(labels, slot, table[slot])
        if k:
            rep_out[k] = answer
            send(8 + k, rep_out.at[k], rep_in.at[k], at.along_y(-k))
        else:
            rep_in[0] = answer

    def put(j, block, position):
        for t in range(TAPS):
            shift = (t // 3 - 1) * 10 + t % 3 - 1
            rolled = pltpu.roll(block, (-shift) % 128, 1) if shift else block
            window[j, t * FINE:(t + 1) * FINE, position * 128:(position + 1) * 128] = rolled.astype(BF16)

    def own_planes(j, carry):
        for n in range(9):
            code = neighbours[j, 9 + n]
            which = jnp.clip(code - BRICKS, 0, BRICKS)
            for p in range(4):
                gathered[p * FINE:(p + 1) * FINE, n * 128:(n + 1) * 128] = (
                    source[which, :, p * 128:(p + 1) * 128])
        planes = mul(gathered[...], pad_m[...])
        for p in range(4):
            for half in range(2):
                put(j, planes[p * FINE:(p + 1) * FINE, half * 128:(half + 1) * 128], 2 * p + half + 1)
        return carry

    lax.fori_loop(0, BRICKS, own_planes, 0)

    link(0, source.at[first, :, last], lower.at[first], below).wait_recv()
    link(1, source.at[first, :, pl.ds(0, 128)], upper.at[first], above).wait_recv()

    def convolve(j, carry):
        for n in range(9):
            low, high = neighbours[j, n], neighbours[j, 18 + n]
            which_low = jnp.clip(low, 0, BRICKS)
            which_high = jnp.clip(high - 2 * BRICKS, 0, BRICKS)
            edge[:, n * 128:(n + 1) * 128] = jnp.where(
                low_lanes((FINE, 128)), upper[which_high], lower[which_low])
        planes = mul(edge[...], pad_m[...])
        put(j, planes[:, :128], 9)
        put(j, planes[:, 128:], 0)
        wide[...] = mul(w_cat[...], window[j])
        total = wide[0:FINE, 0:1024]
        total = total + wide[FINE:2 * FINE, 128:1152]
        total = total + wide[2 * FINE:3 * FINE, 256:1280]
        pre_act = total * occ_pad[pl.ds(j, 1)]
        active[rows_at(j * FINE, FINE)] = jnp.maximum(pre_act, 0.0).astype(BF16)
        return carry

    lax.fori_loop(0, BRICKS, convolve, 0)

    octants = mul(active[...], oct_m[...]).astype(BF16)
    for j in range(BRICKS):
        for pair in range(4):
            act_oct[pair * FINE:(pair + 1) * FINE, j * 128:(j + 1) * 128] = (
                octants[j * FINE:(j + 1) * FINE, pair * 128:(pair + 1) * 128])
    summed = mul(w_pair[...], act_oct[...])
    for j in range(BRICKS):
        even = summed[:COARSE, j * 128:(j + 1) * 128]
        odd = summed[COARSE:, j * 128:(j + 1) * 128]
        both = jnp.where(low_lanes((COARSE, 128)), even, odd)
        both = both + pltpu.roll(both, 64, 1)
        oct_pack[j] = packed(both).astype(BF16)
    oct_pack[BRICKS] = jnp.zeros((64, 128), BF16)
    for k in range(NY):
        block = oct_pack[brick_for((at.y + k) % NY)]
        if k:
            oct_out[k] = block
            send(15 + k, oct_out.at[k], oct_in.at[k], at.along_y(k))
        else:
            oct_in[0] = block

    for k in range(1, NY):
        link(8 + k, rep_out.at[k], rep_in.at[k], at.along_y(k)).wait_recv()
    low = low_lanes((64, 128))
    for j in range(BRICKS):
        block = rep_in[(owner_of[j] - at.y + NY) % NY].astype(F32)
        turned = pltpu.roll(block, 64, 1)
        returned[0:64, j * 128:(j + 1) * 128] = jnp.where(low, block, turned).astype(BF16)
        returned[64:128, j * 128:(j + 1) * 128] = jnp.where(low, turned, block).astype(BF16)
    whole = returned[...].astype(F32)
    low = low_lanes((COARSE, 512))
    ret_half[:COARSE] = jnp.where(low, whole, 0.0).astype(BF16)
    ret_half[COARSE:] = jnp.where(low, 0.0, whole).astype(BF16)
    down = mul(ret_half[...], act_oct[...], NT)
    for b in range(3):
        start = DOWN_START + b * DOWN_ROWS
        grads[start:start + DOWN_ROWS] = down[:, b * 128:(b + 1) * 128]
    grads[USED_ROWS:] = jnp.zeros((grads.shape[0] - USED_ROWS, 128), F32)
    low = low_lanes((FINE, 512))
    for pair in range(4):
        even = mul(w_down[2 * pair], returned[...], TN)
        odd = mul(w_down[2 * pair + 1], returned[...], TN)
        both = jnp.where(low, even, odd).astype(BF16)
        for j in range(BRICKS):
            back[j * FINE:(j + 1) * FINE, pair * 128:(pair + 1) * 128] = both[:, j * 128:(j + 1) * 128]

    shifted[...] = jnp.zeros(shifted.shape, BF16)

    def weight_gradient(j, carry):
        rows = rows_at(j * FINE, FINE)
        grad_act = mul(back[rows], oct_m[...], NT)
        grad_pre = jnp.where(active[rows].astype(F32) > 0, grad_act, 0.0).astype(BF16)
        for kx in range(3):
            shifted[kx * FINE:(kx + 1) * FINE, kx * 128:kx * 128 + 1024] = grad_pre
        part = mul(shifted[...], window[j], NT)

        @pl.when(j == 0)
        def _():
            for b in range(6):
                grads[b * SUB_ROWS:(b + 1) * SUB_ROWS] = part[:, b * 128:(b + 1) * 128]
            grads[6 * SUB_ROWS:7 * SUB_ROWS] = jnp.zeros((SUB_ROWS, 128), F32)
            grads[6 * SUB_ROWS:7 * SUB_ROWS, 0:96] = part[:, 768:864]

        @pl.when(j > 0)
        def _():
            for b in range(6):
                grads[b * SUB_ROWS:(b + 1) * SUB_ROWS] += part[:, b * 128:(b + 1) * 128]
            grads[6 * SUB_ROWS:7 * SUB_ROWS, 0:96] += part[:, 768:864]

        return carry

    lax.fori_loop(0, BRICKS, weight_gradient, 0)

    def place_octants():
        for k in range(1, NY):
            link(15 + k, oct_out.at[k], oct_in.at[k], at.along_y(-k)).wait_recv()
        low = low_lanes((64, 128))
        for slot in range(16):
            s, m = slot // 8, slot % 8
            block = chosen(lab_in[0], slot, oct_in[0])
            for k in range(1, NY):
                block = block + chosen(lab_in[k], slot, oct_in[k])
            block = block.astype(F32)
            lanes = slice(m * 128, (m + 1) * 128)
            place_in[s * 128:s * 128 + 64, lanes] = jnp.where(low, block, 0.0).astype(BF16)
            place_in[s * 128 + 64:s * 128 + 128, lanes] = jnp.where(low, 0.0, block).astype(BF16)
        result = mul(place_in[...], place_m[...]).astype(BF16)
        for s in range(2):
            coarse[s] = result[s * COARSE:(s + 1) * COARSE]

    work.run(grads, place_octants)

    def side_by_side(base, rows, block, start):
        b, offset = start // 128, start % 128
        left = work.total[base + b * block + rows.start:base + b * block + rows.stop].astype(F32)
        if offset:
            left = pltpu.roll(left, 128 - offset, 1)
        if offset > 32:
            right = work.total[base + (b + 1) * block + rows.start:
                               base + (b + 1) * block + rows.stop].astype(F32)
            right = pltpu.roll(right, 128 - offset, 1)
            lane = lax.broadcasted_iota(jnp.int32, left.shape, 1)
            left = jnp.where(lane < 128 - offset, left, right)
        return left[:, :FINE]

    for kx in range(3):
        for t in range(TAPS):
            rows = slice(kx * FINE, (kx + 1) * FINE)
            grad_sub[TAPS * kx + t] = side_by_side(0, rows, SUB_ROWS, t * FINE)
    for octant in range(8):
        rows = slice(octant % 2 * COARSE, (octant % 2 + 1) * COARSE)
        grad_down[octant] = side_by_side(DOWN_START, rows, DOWN_ROWS, octant // 2 * FINE)
    for copy in started:
        copy.wait_send()
    work.finish()


def per_device(sizes, features, occupancy, neighbours, owners, octslots, cotangent, w_sub, w_down):
    vmem = pl.BlockSpec(memory_space=pltpu.VMEM)
    smem = pl.BlockSpec(memory_space=pltpu.SMEM)
    v = pltpu.VMEM
    coarse, grad_sub, grad_down = pl.pallas_call(
        functools.partial(kernel, sizes),
        out_shape=(
            jax.ShapeDtypeStruct(cotangent.shape[1:], BF16),
            jax.ShapeDtypeStruct(w_sub.shape, F32),
            jax.ShapeDtypeStruct(w_down.shape, F32),
        ),
        in_specs=[smem] * 3 + [vmem] * 8,
        out_specs=(vmem, vmem, vmem),
        scratch_shapes=[
            v((BRICKS + 1, FINE, 512), BF16),
            v((BRICKS + 1, FINE, 128), BF16),
            v((BRICKS + 1, FINE, 128), BF16),
            v((4 * FINE, TAPS * 128), BF16),
            v((FINE, TAPS * 128), BF16),
            v((BRICKS, TAPS * FINE, 1280), BF16),
            v((3 * FINE, 1280), F32),
            v((BRICKS, 1024), F32),
            v((BRICKS * FINE, 1024), BF16),
            v((4 * FINE, BRICKS * 128), BF16),
            v((3 * FINE, TAPS * FINE), BF16),
            v((2 * COARSE, 4 * FINE), BF16),
            v((BRICKS + 1, 64, 128), BF16),
            v((NY, 64, 128), BF16),
            v((NY, 64, 128), BF16),
            v((NY, 8, 128), jnp.int32),
            v((NY, 8, 128), jnp.int32),
            v((16, 64, 128), BF16),
            v((NY, 64, 128), BF16),
            v((NY, 64, 128), BF16),
            v((COARSE, BRICKS * 128), BF16),
            v((2 * COARSE, BRICKS * 128), BF16),
            v((BRICKS * FINE, 512), BF16),
            v((3 * FINE, 1280), BF16),
            v((2 * sizes[1] * QUARTER, 128), F32),
            v((2 * COARSE, 1024), BF16),
            pltpu.SemaphoreType.DMA((2 + 3 * (NY - 1),)),
            pltpu.SemaphoreType.DMA((2 + 3 * (NY - 1),)),
        ] + sum_scratch(sizes),
        compiler_params=pltpu.CompilerParams(
            collective_id=0, has_side_effects=True, vmem_limit_bytes=56 * 2**20
        ),
    )(neighbours[0], owners[0], octslots[0], features[0], occupancy[0], cotangent[0], w_sub, w_down,
      jnp.asarray(padding_matrix()), jnp.asarray(octant_matrix()), jnp.asarray(placing_matrix()))
    return coarse[None], grad_sub, grad_down


def solution(mesh):
    sizes = (mesh.shape["space"] // NY, mesh.shape["rep"] // 2)
    return jax.shard_map(
        functools.partial(per_device, sizes),
        mesh=mesh,
        in_specs=(
            P("rep", "space", None, None),
            P("rep", "space", None),
            P("rep", "space", None),
            P("rep", "space"),
            P("rep", "space"),
            P("rep", "space", None, None),
            P(),
            P(),
        ),
        out_specs=(P("rep", "space", None, None), P(), P()),
        check_vma=False,
    )
```

```python
import functools

import jax
import jax.numpy as jnp
import numpy as np
from jax import lax
from jax.experimental import pallas as pl
from jax.experimental.pallas import tpu as pltpu
from jax.sharding import PartitionSpec as P

MESH = pl.DeviceIdType.MESH
F32, BF16 = jnp.float32, jnp.bfloat16
NT = (((1,), (1,)), ((), ()))
NN = (((1,), (0,)), ((), ()))
TN = (((0,), (0,)), ((), ()))
NY = 8
BRICKS = 4
FINE = 96
COARSE = 128
TAPS = 9
PLANES = 640
SUB_ROWS = 3 * FINE
DOWN_ROWS = 4 * FINE
FIRST_BLOCKS = 4
LAST_BLOCKS = 3
FIRST_PIECE = 32
LAST_PIECE = 16
DOWN_START = FIRST_BLOCKS * SUB_ROWS


class Place:
    def __init__(self, sizes):
        self.nz, self.nx = sizes
        space, rep = lax.axis_index("space"), lax.axis_index("rep")
        self.z, self.y = space // NY, space % NY
        self.x, self.core = rep // 2, rep % 2

    def across(self):
        return (self.z * NY + self.y, self.x * 2 + 1 - self.core)

    def along_x(self, k):
        return (self.z * NY + self.y, (self.x + k) % self.nx * 2 + self.core)

    def along_y(self, k):
        return (self.z * NY + (self.y + k) % NY, self.x * 2 + self.core)

    def along_z(self, k):
        return ((self.z + k) % self.nz * NY + self.y, self.x * 2 + self.core)

    def sum_partners(self):
        near = [self.across()]
        near += [self.along_x(k) for k in range(1, self.nx)]
        near += [self.along_y(k) for k in range(1, NY)]
        near += [self.along_z(k) for k in range(1, self.nz)]
        return near


def rows_at(start, count):
    return pl.ds(pl.multiple_of(start, 16), count)


def sum_rows(sizes, piece):
    return 2 * sizes[1] * NY * piece


def sum_scratch(sizes, piece):
    nz, nx = sizes
    quarter = NY * piece
    half = nx * quarter
    copies = 2 * nx + 2 * (nx - 1) + 2 * (NY - 1) + (nz - 1)
    return [
        pltpu.VMEM((2 * half, 128), F32),
        pltpu.VMEM((half, 128), BF16),
        pltpu.VMEM((half, 128), BF16),
        pltpu.VMEM((nx - 1, quarter, 128), BF16),
        pltpu.VMEM((nx - 1, quarter, 128), BF16),
        pltpu.VMEM((quarter, 128), F32),
        pltpu.VMEM((quarter, 128), BF16),
        pltpu.VMEM((NY - 1, piece, 128), BF16),
        pltpu.VMEM((nz, piece, 128), BF16),
        pltpu.VMEM((2 * half, 128), BF16),
        pltpu.SemaphoreType.DMA((copies,)),
        pltpu.SemaphoreType.DMA((copies,)),
        pltpu.SemaphoreType.DMA((2 * nx,)),
    ]


class GradSum:
    def __init__(self, place, piece, scratch, result):
        self.place, self.piece, self.result = place, piece, result
        (self.grads, self.core_out, self.core_in, self.x_out, self.x_in, self.mine, self.y_out,
         self.y_in, self.z_all, self.total, self.send_sem, self.recv_sem, self.save_sem) = scratch
        self.used = 0
        self.sent = []
        self.saved = []

    def slots(self, count):
        self.used += count
        return range(self.used - count, self.used)

    def send(self, slot, src, dst, device):
        copy = pltpu.make_async_remote_copy(
            src_ref=src, dst_ref=dst, send_sem=self.send_sem.at[slot],
            recv_sem=self.recv_sem.at[slot], device_id=device, device_id_type=MESH)
        copy.start()
        self.sent.append(copy)

    def arrive(self, slot, dst, device):
        pltpu.make_async_remote_copy(
            src_ref=dst, dst_ref=dst, send_sem=self.send_sem.at[slot],
            recv_sem=self.recv_sem.at[slot], device_id=device, device_id_type=MESH).wait_recv()

    def save(self, rows):
        copy = pltpu.make_async_copy(
            self.total.at[rows], self.result.at[rows], self.save_sem.at[len(self.saved)])
        copy.start()
        self.saved.append(copy)

    def phases(self):
        at, piece, grads = self.place, self.piece, self.grads
        nx, nz = at.nx, at.nz
        quarter = NY * piece
        half = nx * quarter
        x, y, z, core = at.x, at.y, at.z, at.core

        def part(i):
            return rows_at((x + 1 + i) % nx * quarter, quarter)

        core_slots = self.slots(nx)
        for i in range(nx):
            start = (1 - core) * half + (x + 1 + i) % nx * quarter
            self.core_out[part(i)] = grads[rows_at(start, quarter)].astype(BF16)
            self.send(core_slots[i], self.core_out.at[part(i)], self.core_in.at[part(i)],
                      at.across())
        yield
        x_slots = self.slots(nx - 1)
        for i in range(nx):
            self.arrive(core_slots[i], self.core_in.at[part(i)], at.across())
            start = core * half + (x + 1 + i) % nx * quarter
            pair = grads[rows_at(start, quarter)] + self.core_in[part(i)].astype(F32)
            if i < nx - 1:
                self.x_out[i] = pair.astype(BF16)
                self.send(x_slots[i], self.x_out.at[i], self.x_in.at[i], at.along_x(i + 1))
            else:
                self.mine[...] = pair
        yield
        for i in range(nx - 1):
            self.arrive(x_slots[i], self.x_in.at[i], at.along_x(-i - 1))
            self.mine[...] += self.x_in[i].astype(F32)
        self.y_out[...] = self.mine[...].astype(BF16)
        y_slots = self.slots(NY - 1)
        for k in range(1, NY):
            self.send(y_slots[k - 1], self.y_out.at[rows_at((y + k) % NY * piece, piece)],
                      self.y_in.at[k - 1], at.along_y(k))
        yield
        summed = self.mine[rows_at(y * piece, piece)]
        for k in range(1, NY):
            self.arrive(y_slots[k - 1], self.y_in.at[k - 1], at.along_y(-k))
            summed = summed + self.y_in[k - 1].astype(F32)
        self.z_all[z] = summed.astype(BF16)
        z_slots = self.slots(nz - 1)
        for k in range(1, nz):
            self.send(z_slots[k - 1], self.z_all.at[z], self.z_all.at[z], at.along_z(k))
        yield
        for k in range(1, nz):
            self.arrive(z_slots[k - 1], self.z_all.at[(z - k) % nz], at.along_z(-k))
        summed = self.z_all[0].astype(F32)
        for layer in range(1, nz):
            summed = summed + self.z_all[layer].astype(F32)
        base = core * half + x * quarter

        def piece_rows(k):
            return rows_at(base + (y + k) % NY * piece, piece)

        self.total[piece_rows(0)] = summed.astype(BF16)
        y_slots = self.slots(NY - 1)
        for k in range(1, NY):
            self.send(y_slots[k - 1], self.total.at[piece_rows(0)], self.total.at[piece_rows(0)],
                      at.along_y(k))
        yield
        for k in range(1, NY):
            self.arrive(y_slots[k - 1], self.total.at[piece_rows(-k)], at.along_y(-k))

        def quarter_of(which, k):
            return rows_at(which * half + (x + k) % nx * quarter, quarter)

        x_slots, core_slots = self.slots(nx - 1), self.slots(nx)
        own = self.total.at[quarter_of(core, 0)]
        for k in range(1, nx):
            self.send(x_slots[k - 1], own, own, at.along_x(k))
        self.send(core_slots[0], own, own, at.across())
        self.save(quarter_of(core, 0))
        yield
        for k in range(1, nx):
            other = self.total.at[quarter_of(core, -k)]
            self.arrive(x_slots[k - 1], other, at.along_x(-k))
            self.send(core_slots[k], other, other, at.across())
            self.save(quarter_of(core, -k))
        yield
        for k in range(nx):
            self.arrive(core_slots[k], self.total.at[quarter_of(1 - core, -k)], at.across())
            self.save(quarter_of(1 - core, -k))
        yield

    def finish(self):
        for copy in self.sent:
            copy.wait_send()
        for copy in self.saved:
            copy.wait()


def mul(a, b, dims=NN):
    return lax.dot_general(a, b, dims, preferred_element_type=F32)


def padding_matrix():
    out = np.zeros((9, 2, 8, 8, 2, 128), np.float32)
    sides = ([(7, 0)], [(i, i + 1) for i in range(8)], [(0, 9)])
    for layer_y in range(3):
        for layer_z in range(3):
            for y, to_y in sides[layer_y]:
                for z, to_z in sides[layer_z]:
                    for half in range(2):
                        out[3 * layer_y + layer_z, half, y, z, half, 10 * to_y + to_z] = 1
    return out.reshape(9 * 128, 256).astype(jnp.bfloat16)


def tap_matrix():
    out = np.zeros((2, 128, 9, 2, 8, 8), np.float32)
    for tap in range(9):
        for y in range(8):
            for z in range(8):
                for half in range(2):
                    out[half, 10 * (y + tap // 3) + z + tap % 3, tap, half, y, z] = 1
    return out.reshape(256, 9 * 128).astype(jnp.bfloat16)


def octant_matrix():
    out = np.zeros((8, 8, 8, 8, 64), np.float32)
    for x in range(8):
        for y in range(8):
            for z in range(8):
                octant = x % 2 * 4 + y % 2 * 2 + z % 2
                out[x, y, z, octant, x // 2 * 16 + y // 2 * 4 + z // 2] = 1
    return out.reshape(512, 512).astype(jnp.bfloat16)


def placing_matrix():
    out = np.zeros((8, 2, 64, 8, 8, 8), np.float32)
    for octant in range(8):
        for v in range(64):
            x, y, z = v // 16, v // 4 % 4, v % 4
            spot = (octant // 4 * 4 + x, octant // 2 % 2 * 4 + y, octant % 2 * 4 + z)
            out[(octant, slice(None), v) + spot] = 1
    return out.reshape(1024, 512).astype(jnp.bfloat16)


def low_lanes(shape):
    return lax.broadcasted_iota(jnp.int32, shape, len(shape) - 1) % 128 < 64


def packed(block):
    return jnp.where(low_lanes((64, 128)), block[:64], block[64:])


def chosen(labels, slot, table):
    hit = jnp.where(labels[0:1] == slot, 1.0, 0.0).astype(BF16)
    return hit * table


def kernel(sizes, neighbours, owners, octslots, features, occupancy, *refs):
    held, (out_first, out_last, out_coarse) = refs[:7], refs[7:10]
    loaded, refs = refs[10:17], refs[17:]
    cotangent, w_sub, w_down, pad_m, tap_m, oct_m, place_m = loaded
    (load_sem, source, upper, lower, gathered, edge, window, active, act_oct, w_cat, w_pair,
     oct_pack, oct_out, oct_in, lab_out, lab_in, table, rep_out, rep_in, returned, ret_half,
     back, shifted, place_in, coarse, pair_send, pair_recv) = refs[:27]
    sums = refs[27:]
    at = Place(sizes)
    first_sum = GradSum(at, FIRST_PIECE, sums[:len(sums) // 2], out_first)
    last_sum = GradSum(at, LAST_PIECE, sums[len(sums) // 2:], out_last)
    nspace = at.nz * NY
    me = at.z * NY + at.y
    rep = at.x * 2 + at.core
    above, below = ((me + 1) % nspace, rep), ((me + nspace - 1) % nspace, rep)
    partners = at.sum_partners() + [above, below]
    barrier = pltpu.get_barrier_semaphore()
    for partner in partners:
        pl.semaphore_signal(barrier, inc=1, device_id=partner, device_id_type=MESH)
    loads = [pltpu.make_async_copy(src, dst, load_sem.at[i])
             for i, (src, dst) in enumerate(zip(held, loaded))]
    for copy in loads:
        copy.start()

    def link(slot, src, dst, device):
        return pltpu.make_async_remote_copy(
            src_ref=src, dst_ref=dst, send_sem=pair_send.at[slot], recv_sem=pair_recv.at[slot],
            device_id=device, device_id_type=MESH)

    started = []

    def send(slot, src, dst, device):
        copy = link(slot, src, dst, device)
        copy.start()
        started.append(copy)

    occ = occupancy[...].astype(BF16)
    for j in range(BRICKS):
        source[j] = features[j] * occ[j:j + 1]
    source[BRICKS] = jnp.zeros((FINE, 512), BF16)
    upper[BRICKS] = jnp.zeros((FINE, 128), BF16)
    lower[BRICKS] = jnp.zeros((FINE, 128), BF16)
    owner_of = [owners[j] % NY for j in range(BRICKS)]

    def brick_for(member):
        found = BRICKS
        for j in range(BRICKS):
            found = jnp.where(owner_of[j] == member, j, found)
        return found

    for k in range(NY):
        member = (at.y + k) % NY
        label = -1
        for j in range(BRICKS):
            label = jnp.where(owner_of[j] == member, octslots[j], label)
        lab_out[k] = jnp.full((8, 128), label, jnp.int32)

    pl.semaphore_wait(barrier, len(partners))
    own, head, tail = pl.ds(0, BRICKS), pl.ds(0, 128), pl.ds(384, 128)
    send(0, source.at[own, :, tail], lower.at[own], above)
    send(1, source.at[own, :, head], upper.at[own], below)
    for k in range(1, NY):
        send(1 + k, lab_out.at[k], lab_in.at[k], at.along_y(k))
    lab_in[0] = lab_out[0]

    for copy in loads:
        copy.wait()
    spread = mul(cotangent[...].reshape(2 * COARSE, 512), place_m[...], NT)
    for s in range(2):
        for m in range(8):
            block = spread[s * COARSE:(s + 1) * COARSE, m * 128:(m + 1) * 128]
            table[8 * s + m] = packed(block).astype(BF16)
    for kx in range(3):
        w_cat[kx * FINE:(kx + 1) * FINE] = jnp.concatenate(
            [w_sub[TAPS * kx + t] for t in range(TAPS)], axis=1)
    for pair in range(4):
        for parity in range(2):
            w_pair[pair * FINE:(pair + 1) * FINE, parity * 128:(parity + 1) * 128] = (
                w_down[2 * pair + parity])

    for k in range(NY):
        if k:
            link(1 + k, lab_out.at[k], lab_in.at[k], at.along_y(-k)).wait_recv()
        labels = lab_in[k]
        answer = chosen(labels, 0, table[0])
        for slot in range(1, 16):
            answer = answer + chosen(labels, slot, table[slot])
        if k:
            rep_out[k] = answer
            send(8 + k, rep_out.at[k], rep_in.at[k], at.along_y(-k))
        else:
            rep_in[0] = answer

    for j in range(BRICKS):
        for n in range(9):
            which = jnp.clip(neighbours[j, 9 + n] - BRICKS, 0, BRICKS)
            for p in range(4):
                row = (j * 4 + p) * FINE
                gathered[row:row + FINE, n * 128:(n + 1) * 128] = (
                    source[which, :, p * 128:(p + 1) * 128])
    planes = mul(gathered[...], pad_m[...]).astype(BF16)
    planes = mul(planes, tap_m[...]).astype(BF16)
    for j in range(BRICKS):
        for p in range(4):
            row, column = (j * 4 + p) * FINE, j * PLANES + p * 128
            for t in range(TAPS):
                window[t * FINE:(t + 1) * FINE, column:column + 128] = (
                    planes[row:row + FINE, t * 128:(t + 1) * 128])

    link(0, source.at[own, :, tail], lower.at[own], below).wait_recv()
    link(1, source.at[own, :, head], upper.at[own], above).wait_recv()
    low = low_lanes((FINE, 128))
    for j in range(BRICKS):
        for n in range(9):
            which_low = jnp.clip(neighbours[j, n], 0, BRICKS)
            which_high = jnp.clip(neighbours[j, 18 + n] - 2 * BRICKS, 0, BRICKS)
            edge[j * FINE:(j + 1) * FINE, n * 128:(n + 1) * 128] = jnp.where(
                low, upper[which_high], lower[which_low])
    planes = mul(edge[...], pad_m[...]).astype(BF16)
    planes = mul(planes, tap_m[...]).astype(BF16)
    for j in range(BRICKS):
        column = j * PLANES + 512
        for t in range(TAPS):
            window[t * FINE:(t + 1) * FINE, column:column + 128] = (
                planes[j * FINE:(j + 1) * FINE, t * 128:(t + 1) * 128])

    def turned(rows):
        return [pltpu.roll(rows[:, i * 128:(i + 1) * 128], 64, 1) for i in range(rows.shape[1] // 128)]

    for two in range(BRICKS // 2):
        columns = slice(2 * two * PLANES, 2 * (two + 1) * PLANES)
        wide = mul(w_cat[...], window[:, columns])
        for j in (2 * two, 2 * two + 1):
            brick = wide[:, j % 2 * PLANES:(j % 2 + 1) * PLANES]
            behind, ahead = turned(brick[:FINE]), turned(brick[2 * FINE:])
            for i in range(4):
                lanes = slice(i * 128, (i + 1) * 128)
                total = brick[FINE:2 * FINE, lanes]
                total = total + jnp.where(low, ahead[i], ahead[i + 1])
                total = total + jnp.where(low, behind[i - 1], behind[i])
                pre_act = total * occupancy[j:j + 1, lanes].astype(F32)
                active[j * FINE:(j + 1) * FINE, lanes] = jnp.maximum(pre_act, 0.0).astype(BF16)

    octants = mul(active[...], oct_m[...]).astype(BF16)
    for j in range(BRICKS):
        for pair in range(4):
            act_oct[pair * FINE:(pair + 1) * FINE, j * 128:(j + 1) * 128] = (
                octants[j * FINE:(j + 1) * FINE, pair * 128:(pair + 1) * 128])
    summed = mul(w_pair[...], act_oct[...], TN)
    for j in range(BRICKS):
        even = summed[:COARSE, j * 128:(j + 1) * 128]
        odd = summed[COARSE:, j * 128:(j + 1) * 128]
        both = jnp.where(low_lanes((COARSE, 128)), even, odd)
        both = both + pltpu.roll(both, 64, 1)
        oct_pack[j] = packed(both).astype(BF16)
    oct_pack[BRICKS] = jnp.zeros((64, 128), BF16)
    for k in range(NY):
        block = oct_pack[brick_for((at.y + k) % NY)]
        if k:
            oct_out[k] = block
            send(15 + k, oct_out.at[k], oct_in.at[k], at.along_y(k))
        else:
            oct_in[0] = block

    for k in range(1, NY):
        link(8 + k, rep_out.at[k], rep_in.at[k], at.along_y(k)).wait_recv()
    low_rows = low_lanes((64, 128))
    for j in range(BRICKS):
        block = rep_in[(owner_of[j] - at.y + NY) % NY].astype(F32)
        other = pltpu.roll(block, 64, 1)
        returned[0:64, j * 128:(j + 1) * 128] = jnp.where(low_rows, block, other).astype(BF16)
        returned[64:128, j * 128:(j + 1) * 128] = jnp.where(low_rows, other, block).astype(BF16)
    whole = returned[...].astype(F32)
    low_half = low_lanes((COARSE, 512))
    ret_half[:COARSE] = jnp.where(low_half, whole, 0.0).astype(BF16)
    ret_half[COARSE:] = jnp.where(low_half, 0.0, whole).astype(BF16)
    spread = mul(w_down[...].reshape(8 * FINE, COARSE), returned[...])
    low_half = low_lanes((FINE, 512))
    for pair in range(4):
        even = spread[2 * pair * FINE:(2 * pair + 1) * FINE]
        odd = spread[(2 * pair + 1) * FINE:(2 * pair + 2) * FINE]
        both = jnp.where(low_half, even, odd).astype(BF16)
        for j in range(BRICKS):
            back[j * FINE:(j + 1) * FINE, pair * 128:(pair + 1) * 128] = both[:, j * 128:(j + 1) * 128]
    grad_act = mul(back[...], oct_m[...], NT)
    grad_pre = jnp.where(active[...].astype(F32) > 0, grad_act, 0.0)
    for j in range(BRICKS):
        brick = grad_pre[j * FINE:(j + 1) * FINE]
        sides = turned(brick) + [jnp.zeros((FINE, 128), F32)]
        for i in range(5):
            lanes = slice(j * PLANES + i * 128, j * PLANES + (i + 1) * 128)
            middle = brick[:, i * 128:(i + 1) * 128] if i < 4 else sides[4]
            shifted[0:FINE, lanes] = jnp.where(low, sides[i], sides[(i + 1) % 5]).astype(BF16)
            shifted[FINE:2 * FINE, lanes] = middle.astype(BF16)
            shifted[2 * FINE:, lanes] = jnp.where(low, sides[i - 1], sides[i]).astype(BF16)

    split = FIRST_BLOCKS * 128
    part = mul(shifted[...], window[0:split], NT)
    for b in range(FIRST_BLOCKS):
        first_sum.grads[b * SUB_ROWS:(b + 1) * SUB_ROWS] = part[:, b * 128:(b + 1) * 128]
    part = mul(act_oct[...], ret_half[...], NT)
    for parity in range(2):
        start = DOWN_START + parity * DOWN_ROWS
        first_sum.grads[start:start + DOWN_ROWS] = part[:, parity * 128:(parity + 1) * 128]
    used = DOWN_START + 2 * DOWN_ROWS
    first_sum.grads[used:] = jnp.zeros((first_sum.grads.shape[0] - used, 128), F32)
    first = first_sum.phases()
    next(first)
    last_sum.grads[...] = jnp.zeros(last_sum.grads.shape, F32)
    part = mul(shifted[...], window[split:], NT)
    for b in range(LAST_BLOCKS):
        width = min(128, TAPS * FINE - split - b * 128)
        last_sum.grads[b * SUB_ROWS:(b + 1) * SUB_ROWS, 0:width] = part[:, b * 128:b * 128 + width]
    last = last_sum.phases()
    next(last)

    def place_octants():
        for k in range(1, NY):
            link(15 + k, oct_out.at[k], oct_in.at[k], at.along_y(-k)).wait_recv()
        for slot in range(16):
            s, m = slot // 8, slot % 8
            block = chosen(lab_in[0], slot, oct_in[0])
            for k in range(1, NY):
                block = block + chosen(lab_in[k], slot, oct_in[k])
            block = block.astype(F32)
            lanes = slice(m * 128, (m + 1) * 128)
            place_in[s * 128:s * 128 + 64, lanes] = jnp.where(low_rows, block, 0.0).astype(BF16)
            place_in[s * 128 + 64:s * 128 + 128, lanes] = jnp.where(low_rows, 0.0, block).astype(BF16)
        result = mul(place_in[...], place_m[...]).astype(BF16)
        for s in range(2):
            coarse[s] = result[s * COARSE:(s + 1) * COARSE]

    save = pltpu.make_async_copy(coarse, out_coarse, load_sem.at[len(loads)])
    for phase in range(1, 8):
        next(first)
        next(last)
        if phase == 2:
            place_octants()
            save.start()
    for copy in started:
        copy.wait_send()
    first_sum.finish()
    last_sum.finish()
    save.wait()


def unpack_kernel(first, last, coarse_in, coarse, grad_sub, grad_down, sub, down, sems):
    copies = [pltpu.make_async_copy(coarse_in, coarse, sems.at[0])]
    copies[0].start()
    for octant in range(8):
        row = DOWN_START + octant % 2 * DOWN_ROWS + octant // 2 * FINE
        down[octant] = first[row:row + FINE].astype(F32)
    copies.append(pltpu.make_async_copy(down, grad_down, sems.at[1]))
    copies[-1].start()

    def block(b, kx):
        ref, b = (first, b) if b < FIRST_BLOCKS else (last, b - FIRST_BLOCKS)
        row = b * SUB_ROWS + kx * FINE
        return ref[row:row + FINE].astype(F32)

    lane = lax.broadcasted_iota(jnp.int32, (FINE, 128), 1)
    for kx in range(3):
        for t in range(TAPS):
            b, offset = t * FINE // 128, t * FINE % 128
            left = block(b, kx)
            if offset:
                left = pltpu.roll(left, 128 - offset, 1)
            if offset > 32:
                right = pltpu.roll(block(b + 1, kx), 128 - offset, 1)
                left = jnp.where(lane < 128 - offset, left, right)
            sub[TAPS * kx + t] = left[:, :FINE]
        taps = pl.ds(TAPS * kx, TAPS)
        copies.append(pltpu.make_async_copy(sub.at[taps], grad_sub.at[taps], sems.at[2 + kx]))
        copies[-1].start()
    for copy in copies:
        copy.wait()


def per_device(sizes, features, occupancy, neighbours, owners, octslots, cotangent, w_sub, w_down):
    vmem = pl.BlockSpec(memory_space=pltpu.VMEM)
    smem = pl.BlockSpec(memory_space=pltpu.SMEM)
    hbm = pl.BlockSpec(memory_space=pl.ANY)
    v = pltpu.VMEM
    held = [cotangent[0], w_sub, jnp.transpose(w_down, (0, 2, 1)), jnp.asarray(padding_matrix()),
            jnp.asarray(tap_matrix()), jnp.asarray(octant_matrix()), jnp.asarray(placing_matrix())]
    rows = [sum_rows(sizes, piece) for piece in (FIRST_PIECE, LAST_PIECE)]
    first, last, coarse = pl.pallas_call(
        functools.partial(kernel, sizes),
        out_shape=(
            jax.ShapeDtypeStruct((rows[0], 128), BF16),
            jax.ShapeDtypeStruct((rows[1], 128), BF16),
            jax.ShapeDtypeStruct(cotangent.shape[1:], BF16),
        ),
        in_specs=[smem] * 3 + [vmem] * 2 + [hbm] * 7,
        out_specs=(hbm, hbm, hbm),
        scratch_shapes=[v(a.shape, a.dtype) for a in held] + [
            pltpu.SemaphoreType.DMA((8,)),
            v((BRICKS + 1, FINE, 512), BF16),
            v((BRICKS + 1, FINE, 128), BF16),
            v((BRICKS + 1, FINE, 128), BF16),
            v((BRICKS * 4 * FINE, TAPS * 128), BF16),
            v((BRICKS * FINE, TAPS * 128), BF16),
            v((TAPS * FINE, BRICKS * PLANES), BF16),
            v((BRICKS * FINE, 512), BF16),
            v((4 * FINE, BRICKS * 128), BF16),
            v((3 * FINE, TAPS * FINE), BF16),
            v((4 * FINE, 2 * COARSE), BF16),
            v((BRICKS + 1, 64, 128), BF16),
            v((NY, 64, 128), BF16),
            v((NY, 64, 128), BF16),
            v((NY, 8, 128), jnp.int32),
            v((NY, 8, 128), jnp.int32),
            v((16, 64, 128), BF16),
            v((NY, 64, 128), BF16),
            v((NY, 64, 128), BF16),
            v((COARSE, BRICKS * 128), BF16),
            v((2 * COARSE, BRICKS * 128), BF16),
            v((BRICKS * FINE, 512), BF16),
            v((3 * FINE, BRICKS * PLANES), BF16),
            v((2 * COARSE, 1024), BF16),
            v((2, COARSE, 512), BF16),
            pltpu.SemaphoreType.DMA((2 + 3 * (NY - 1),)),
            pltpu.SemaphoreType.DMA((2 + 3 * (NY - 1),)),
        ] + sum_scratch(sizes, FIRST_PIECE) + sum_scratch(sizes, LAST_PIECE),
        compiler_params=pltpu.CompilerParams(
            collective_id=0, has_side_effects=True, vmem_limit_bytes=56 * 2**20
        ),
    )(neighbours[0], owners[0], octslots[0], features[0], occupancy[0], *held)
    coarse, grad_sub, grad_down = pl.pallas_call(
        unpack_kernel,
        out_shape=(
            jax.ShapeDtypeStruct(cotangent.shape[1:], BF16),
            jax.ShapeDtypeStruct(w_sub.shape, F32),
            jax.ShapeDtypeStruct((8, FINE, COARSE), F32),
        ),
        in_specs=[vmem, vmem, hbm],
        out_specs=(hbm, hbm, hbm),
        scratch_shapes=[
            v(w_sub.shape, F32),
            v((8, FINE, COARSE), F32),
            pltpu.SemaphoreType.DMA((5,)),
        ],
        compiler_params=pltpu.CompilerParams(vmem_limit_bytes=32 * 2**20),
    )(first, last, coarse)
    return coarse[None], grad_sub, jnp.transpose(grad_down, (0, 2, 1))


def solution(mesh):
    sizes = (mesh.shape["space"] // NY, mesh.shape["rep"] // 2)
    return jax.shard_map(
        functools.partial(per_device, sizes),
        mesh=mesh,
        in_specs=(
            P("rep", "space", None, None),
            P("rep", "space", None),
            P("rep", "space", None),
            P("rep", "space"),
            P("rep", "space"),
            P("rep", "space", None, None),
            P(),
            P(),
        ),
        out_specs=(P("rep", "space", None, None), P(), P()),
        check_vma=False,
    )
```

```python
import functools

import jax
import jax.numpy as jnp
import numpy as np
from jax import lax
from jax.experimental import pallas as pl
from jax.experimental.pallas import tpu as pltpu
from jax.sharding import PartitionSpec as P

MESH = pl.DeviceIdType.MESH
F32, BF16 = jnp.float32, jnp.bfloat16
NT = (((1,), (1,)), ((), ()))
NN = (((1,), (0,)), ((), ()))
TN = (((0,), (0,)), ((), ()))
NY = 8
BRICKS = 4
FINE = 96
COARSE = 128
TAPS = 9
PLANES = 640
SUB_ROWS = 3 * FINE
DOWN_ROWS = 4 * FINE
SUB_BLOCKS = 7
FIRST_PIECE = 32
LAST_PIECE = 16
FIRST_ORDER, LAST_ORDER = "xyz", "yxz"


class Place:
    def __init__(self, sizes):
        self.nz, self.nx = sizes
        space, rep = lax.axis_index("space"), lax.axis_index("rep")
        self.z, self.y = space // NY, space % NY
        self.x, self.core = rep // 2, rep % 2

    def across(self):
        return (self.z * NY + self.y, self.x * 2 + 1 - self.core)

    def along_x(self, k):
        return (self.z * NY + self.y, (self.x + k) % self.nx * 2 + self.core)

    def along_y(self, k):
        return (self.z * NY + (self.y + k) % NY, self.x * 2 + self.core)

    def along_z(self, k):
        return ((self.z + k) % self.nz * NY + self.y, self.x * 2 + self.core)

    def sum_partners(self):
        far = [self.along_y(k) for k in far_first(NY)]
        far += [self.along_z(k) for k in far_first(self.nz)]
        far += [self.along_x(k) for k in far_first(self.nx)]
        return far + [self.across()]


def rows_at(start, count):
    return pl.ds(pl.multiple_of(start, 16), count)


def near_first(count):
    return sorted(range(1, count), key=lambda k: min(k, count - k))


def far_first(count):
    return near_first(count)[::-1]


def sum_rows(sizes, piece):
    return 2 * sizes[1] * NY * piece


def axis_sizes(sizes, order):
    return [{"x": sizes[1], "y": NY, "z": sizes[0]}[axis] for axis in order]


def sum_scratch(sizes, piece, order):
    na, nb, nc = axis_sizes(sizes, order)
    share = nb * piece
    half = na * share
    copies = 2 * na + 2 * (na - 1) + 2 * (nb - 1) + (nc - 1)
    return [
        pltpu.VMEM((2 * half, 128), F32),
        pltpu.VMEM((half, 128), BF16),
        pltpu.VMEM((half, 128), BF16),
        pltpu.VMEM((na - 1, share, 128), BF16),
        pltpu.VMEM((na - 1, share, 128), BF16),
        pltpu.VMEM((share, 128), F32),
        pltpu.VMEM((share, 128), BF16),
        pltpu.VMEM((nb - 1, piece, 128), BF16),
        pltpu.VMEM((nc, piece, 128), BF16),
        pltpu.VMEM((2 * half, 128), BF16),
        pltpu.SemaphoreType.DMA((copies,)),
        pltpu.SemaphoreType.DMA((copies,)),
        pltpu.SemaphoreType.DMA((2 * na,)),
    ]


class GradSum:
    def __init__(self, place, piece, order, scratch, result):
        self.place, self.piece, self.order, self.result = place, piece, order, result
        (self.grads, self.core_out, self.core_in, self.a_out, self.a_in, self.mine, self.b_out,
         self.b_in, self.c_all, self.total, self.send_sem, self.recv_sem, self.save_sem) = scratch
        self.used = 0
        self.sent = []
        self.saved = []

    def slots(self, count):
        self.used += count
        return range(self.used - count, self.used)

    def send(self, slot, src, dst, device):
        copy = pltpu.make_async_remote_copy(
            src_ref=src, dst_ref=dst, send_sem=self.send_sem.at[slot],
            recv_sem=self.recv_sem.at[slot], device_id=device, device_id_type=MESH)
        copy.start()
        self.sent.append(copy)

    def arrive(self, slot, dst, device):
        pltpu.make_async_remote_copy(
            src_ref=dst, dst_ref=dst, send_sem=self.send_sem.at[slot],
            recv_sem=self.recv_sem.at[slot], device_id=device, device_id_type=MESH).wait_recv()

    def save(self, rows):
        save = pltpu.make_async_copy(
            self.total.at[rows], self.result.at[rows], self.save_sem.at[len(self.saved)])
        save.start()
        self.saved.append(save)

    def phases(self):
        at, piece, grads = self.place, self.piece, self.grads
        na, nb, nc = axis_sizes((at.nz, at.nx), self.order)
        a, b, c = [{"x": at.x, "y": at.y, "z": at.z}[axis] for axis in self.order]
        along_a, along_b, along_c = [
            {"x": at.along_x, "y": at.along_y, "z": at.along_z}[axis] for axis in self.order]
        share = nb * piece
        half = na * share
        core = at.core

        def part(k):
            return rows_at((a + k) % na * share, share)

        core_slots = self.slots(na)
        for k in far_first(na) + [0]:
            start = (1 - core) * half + (a + k) % na * share
            self.core_out[part(k)] = grads[rows_at(start, share)].astype(BF16)
            self.send(core_slots[k], self.core_out.at[part(k)], self.core_in.at[part(k)],
                      at.across())
        yield
        a_slots = self.slots(na - 1)
        for k in far_first(na) + [0]:
            self.arrive(core_slots[k], self.core_in.at[part(k)], at.across())
            start = core * half + (a + k) % na * share
            pair = grads[rows_at(start, share)] + self.core_in[part(k)].astype(F32)
            if k:
                self.a_out[k - 1] = pair.astype(BF16)
                self.send(a_slots[k - 1], self.a_out.at[k - 1], self.a_in.at[k - 1], along_a(k))
            else:
                self.mine[...] = pair
        yield
        summed = self.mine[...]
        for k in near_first(na):
            self.arrive(a_slots[k - 1], self.a_in.at[k - 1], along_a(-k))
            summed = summed + self.a_in[k - 1].astype(F32)
        self.mine[...] = summed
        self.b_out[...] = summed.astype(BF16)
        b_slots = self.slots(nb - 1)
        for k in far_first(nb):
            self.send(b_slots[k - 1], self.b_out.at[rows_at((b + k) % nb * piece, piece)],
                      self.b_in.at[k - 1], along_b(k))
        yield
        summed = self.mine[rows_at(b * piece, piece)]
        for k in near_first(nb):
            self.arrive(b_slots[k - 1], self.b_in.at[k - 1], along_b(-k))
            summed = summed + self.b_in[k - 1].astype(F32)
        self.c_all[c] = summed.astype(BF16)
        c_slots = self.slots(nc - 1)
        for k in far_first(nc):
            self.send(c_slots[k - 1], self.c_all.at[c], self.c_all.at[c], along_c(k))
        yield
        for k in near_first(nc):
            self.arrive(c_slots[k - 1], self.c_all.at[(c - k) % nc], along_c(-k))
        summed = self.c_all[0].astype(F32)
        for layer in range(1, nc):
            summed = summed + self.c_all[layer].astype(F32)
        base = core * half + a * share

        def piece_rows(k):
            return rows_at(base + (b + k) % nb * piece, piece)

        self.total[piece_rows(0)] = summed.astype(BF16)
        b_slots = self.slots(nb - 1)
        for k in far_first(nb):
            self.send(b_slots[k - 1], self.total.at[piece_rows(0)], self.total.at[piece_rows(0)],
                      along_b(k))
        yield
        for k in near_first(nb):
            self.arrive(b_slots[k - 1], self.total.at[piece_rows(-k)], along_b(-k))

        def share_of(which, k):
            return rows_at(which * half + (a + k) % na * share, share)

        a_slots, core_slots = self.slots(na - 1), self.slots(na)
        own = self.total.at[share_of(core, 0)]
        for k in far_first(na):
            self.send(a_slots[k - 1], own, own, along_a(k))
        self.send(core_slots[0], own, own, at.across())
        self.save(share_of(core, 0))
        yield
        for k in near_first(na):
            other = self.total.at[share_of(core, -k)]
            self.arrive(a_slots[k - 1], other, along_a(-k))
            self.send(core_slots[k], other, other, at.across())
            self.save(share_of(core, -k))
        yield
        for k in [0] + near_first(na):
            self.arrive(core_slots[k], self.total.at[share_of(1 - core, -k)], at.across())
            self.save(share_of(1 - core, -k))
        yield

    def finish(self):
        for copy in self.sent:
            copy.wait_send()
        for save in self.saved:
            save.wait()


def mul(a, b, dims=NN):
    return lax.dot_general(a, b, dims, preferred_element_type=F32)


def padding_matrix():
    out = np.zeros((9, 2, 8, 8, 2, 128), np.float32)
    sides = ([(7, 0)], [(i, i + 1) for i in range(8)], [(0, 9)])
    for layer_y in range(3):
        for layer_z in range(3):
            for y, to_y in sides[layer_y]:
                for z, to_z in sides[layer_z]:
                    for half in range(2):
                        out[3 * layer_y + layer_z, half, y, z, half, 10 * to_y + to_z] = 1
    return out.reshape(9 * 128, 256).astype(jnp.bfloat16)


def tap_matrix():
    out = np.zeros((2, 128, 9, 2, 8, 8), np.float32)
    for tap in range(9):
        for y in range(8):
            for z in range(8):
                for half in range(2):
                    out[half, 10 * (y + tap // 3) + z + tap % 3, tap, half, y, z] = 1
    return out.reshape(256, 9 * 128).astype(jnp.bfloat16)


def octant_matrix():
    out = np.zeros((8, 8, 8, 8, 64), np.float32)
    for x in range(8):
        for y in range(8):
            for z in range(8):
                octant = x % 2 * 4 + y % 2 * 2 + z % 2
                out[x, y, z, octant, x // 2 * 16 + y // 2 * 4 + z // 2] = 1
    return out.reshape(512, 512).astype(jnp.bfloat16)


def placing_matrix():
    out = np.zeros((8, 2, 64, 8, 8, 8), np.float32)
    for octant in range(8):
        for v in range(64):
            x, y, z = v // 16, v // 4 % 4, v % 4
            spot = (octant // 4 * 4 + x, octant // 2 % 2 * 4 + y, octant % 2 * 4 + z)
            out[(octant, slice(None), v) + spot] = 1
    return out.reshape(1024, 512).astype(jnp.bfloat16)


def low_lanes(shape):
    return lax.broadcasted_iota(jnp.int32, shape, len(shape) - 1) % 128 < 64


def packed(block):
    return jnp.where(low_lanes((64, 128)), block[:64], block[64:])


def chosen(labels, slot, table):
    hit = jnp.where(labels[0:1] == slot, 1.0, 0.0).astype(BF16)
    return hit * table


def kernel(sizes, neighbours, owners, octslots, *refs):
    held, (out_first, out_last, out_coarse) = refs[:9], refs[9:12]
    loaded, refs = refs[12:21], refs[21:]
    features, occupancy, pad_m, tap_m, cotangent, place_m, w_sub, w_down, oct_m = loaded
    (load_sem, source, upper, lower, gathered, edge, window, active, act_oct, w_cat, w_pair,
     oct_pack, oct_out, oct_in, lab_out, lab_in, table, rep_out, rep_in, returned, ret_half,
     back, shifted, place_in, coarse, pair_send, pair_recv) = refs[:27]
    sums = refs[27:]
    at = Place(sizes)
    first_sum = GradSum(at, FIRST_PIECE, FIRST_ORDER, sums[:len(sums) // 2], out_first)
    last_sum = GradSum(at, LAST_PIECE, LAST_ORDER, sums[len(sums) // 2:], out_last)
    nspace = at.nz * NY
    me = at.z * NY + at.y
    rep = at.x * 2 + at.core
    above, below = ((me + 1) % nspace, rep), ((me + nspace - 1) % nspace, rep)
    partners = at.sum_partners() + [above, below]
    barrier = pltpu.get_barrier_semaphore()
    for partner in partners:
        pl.semaphore_signal(barrier, inc=1, device_id=partner, device_id_type=MESH)
    loads = [pltpu.make_async_copy(src, dst, load_sem.at[i])
             for i, (src, dst) in enumerate(zip(held, loaded))]
    for load in loads:
        load.start()

    def link(slot, src, dst, device):
        return pltpu.make_async_remote_copy(
            src_ref=src, dst_ref=dst, send_sem=pair_send.at[slot], recv_sem=pair_recv.at[slot],
            device_id=device, device_id_type=MESH)

    started = []

    def send(slot, src, dst, device):
        copy = link(slot, src, dst, device)
        copy.start()
        started.append(copy)

    for load in loads[:2]:
        load.wait()
    occ = occupancy[...].astype(BF16)
    for j in range(BRICKS):
        source[j] = features[j] * occ[j:j + 1]
    source[BRICKS] = jnp.zeros((FINE, 512), BF16)
    upper[BRICKS] = jnp.zeros((FINE, 128), BF16)
    lower[BRICKS] = jnp.zeros((FINE, 128), BF16)
    owner_of = [owners[j] % NY for j in range(BRICKS)]

    def brick_for(member):
        found = BRICKS
        for j in range(BRICKS):
            found = jnp.where(owner_of[j] == member, j, found)
        return found

    for k in range(NY):
        member = (at.y + k) % NY
        label = -1
        for j in range(BRICKS):
            label = jnp.where(owner_of[j] == member, octslots[j], label)
        lab_out[k] = jnp.full((8, 128), label, jnp.int32)

    first_sum.grads[(SUB_BLOCKS - 1) * SUB_ROWS:] = jnp.zeros(
        (first_sum.grads.shape[0] - (SUB_BLOCKS - 1) * SUB_ROWS, 128), F32)
    last_sum.grads[2 * DOWN_ROWS:] = jnp.zeros((last_sum.grads.shape[0] - 2 * DOWN_ROWS, 128), F32)

    def own_planes(bricks):
        for j in bricks:
            for n in range(9):
                which = jnp.clip(neighbours[j, 9 + n] - BRICKS, 0, BRICKS)
                for p in range(4):
                    row = (j * 4 + p) * FINE
                    gathered[row:row + FINE, n * 128:(n + 1) * 128] = (
                        source[which, :, p * 128:(p + 1) * 128])
        start = bricks[0] * 4 * FINE
        planes = mul(gathered[start:start + len(bricks) * 4 * FINE], pad_m[...]).astype(BF16)
        planes = mul(planes, tap_m[...]).astype(BF16)
        for j in bricks:
            for p in range(4):
                row, column = (j * 4 + p) * FINE - start, j * PLANES + p * 128
                for t in range(TAPS):
                    window[t * FINE:(t + 1) * FINE, column:column + 128] = (
                        planes[row:row + FINE, t * 128:(t + 1) * 128])

    for load in loads[2:4]:
        load.wait()
    own_planes(range(2))
    pl.semaphore_wait(barrier, len(partners))
    own, head, tail = pl.ds(0, BRICKS), pl.ds(0, 128), pl.ds(384, 128)
    for k in far_first(NY):
        send(1 + k, lab_out.at[k], lab_in.at[k], at.along_y(k))
    send(0, source.at[own, :, tail], lower.at[own], above)
    send(1, source.at[own, :, head], upper.at[own], below)
    lab_in[0] = lab_out[0]

    own_planes(range(2, BRICKS))
    for load in loads[4:]:
        load.wait()
    spread = mul(cotangent[...].reshape(2 * COARSE, 512), place_m[...], NT)
    for s in range(2):
        for m in range(8):
            block = spread[s * COARSE:(s + 1) * COARSE, m * 128:(m + 1) * 128]
            table[8 * s + m] = packed(block).astype(BF16)
    for kx in range(3):
        w_cat[kx * FINE:(kx + 1) * FINE] = jnp.concatenate(
            [w_sub[TAPS * kx + t] for t in range(TAPS)], axis=1)
    for pair in range(4):
        for parity in range(2):
            w_pair[pair * FINE:(pair + 1) * FINE, parity * 128:(parity + 1) * 128] = (
                w_down[2 * pair + parity])

    for k in [0] + near_first(NY):
        if k:
            link(1 + k, lab_out.at[k], lab_in.at[k], at.along_y(-k)).wait_recv()
        labels = lab_in[k]
        answer = chosen(labels, 0, table[0])
        for slot in range(1, 16):
            answer = answer + chosen(labels, slot, table[slot])
        if k:
            rep_out[k] = answer
            send(8 + k, rep_out.at[k], rep_in.at[k], at.along_y(-k))
        else:
            rep_in[0] = answer

    link(0, source.at[own, :, tail], lower.at[own], below).wait_recv()
    link(1, source.at[own, :, head], upper.at[own], above).wait_recv()
    low = low_lanes((FINE, 128))
    for j in range(BRICKS):
        for n in range(9):
            which_low = jnp.clip(neighbours[j, n], 0, BRICKS)
            which_high = jnp.clip(neighbours[j, 18 + n] - 2 * BRICKS, 0, BRICKS)
            edge[j * FINE:(j + 1) * FINE, n * 128:(n + 1) * 128] = jnp.where(
                low, upper[which_high], lower[which_low])
    planes = mul(edge[...], pad_m[...]).astype(BF16)
    planes = mul(planes, tap_m[...]).astype(BF16)
    for j in range(BRICKS):
        column = j * PLANES + 512
        for t in range(TAPS):
            window[t * FINE:(t + 1) * FINE, column:column + 128] = (
                planes[j * FINE:(j + 1) * FINE, t * 128:(t + 1) * 128])

    def turned(rows):
        return [pltpu.roll(rows[:, i * 128:(i + 1) * 128], 64, 1) for i in range(rows.shape[1] // 128)]

    for two in range(BRICKS // 2):
        columns = slice(2 * two * PLANES, 2 * (two + 1) * PLANES)
        wide = mul(w_cat[...], window[:, columns])
        for j in (2 * two, 2 * two + 1):
            brick = wide[:, j % 2 * PLANES:(j % 2 + 1) * PLANES]
            behind, ahead = turned(brick[:FINE]), turned(brick[2 * FINE:])
            for i in range(4):
                lanes = slice(i * 128, (i + 1) * 128)
                total = brick[FINE:2 * FINE, lanes]
                total = total + jnp.where(low, ahead[i], ahead[i + 1])
                total = total + jnp.where(low, behind[i - 1], behind[i])
                pre_act = total * occupancy[j:j + 1, lanes].astype(F32)
                active[j * FINE:(j + 1) * FINE, lanes] = jnp.maximum(pre_act, 0.0).astype(BF16)

    octants = mul(active[...], oct_m[...]).astype(BF16)
    for j in range(BRICKS):
        for pair in range(4):
            act_oct[pair * FINE:(pair + 1) * FINE, j * 128:(j + 1) * 128] = (
                octants[j * FINE:(j + 1) * FINE, pair * 128:(pair + 1) * 128])
    summed = mul(w_pair[...], act_oct[...], TN)
    for j in range(BRICKS):
        even = summed[:COARSE, j * 128:(j + 1) * 128]
        odd = summed[COARSE:, j * 128:(j + 1) * 128]
        both = jnp.where(low_lanes((COARSE, 128)), even, odd)
        both = both + pltpu.roll(both, 64, 1)
        oct_pack[j] = packed(both).astype(BF16)
    oct_pack[BRICKS] = jnp.zeros((64, 128), BF16)
    for k in far_first(NY) + [0]:
        block = oct_pack[brick_for((at.y + k) % NY)]
        if k:
            oct_out[k] = block
            send(15 + k, oct_out.at[k], oct_in.at[k], at.along_y(k))
        else:
            oct_in[0] = block

    for k in range(1, NY):
        link(8 + k, rep_out.at[k], rep_in.at[k], at.along_y(k)).wait_recv()
    low_rows = low_lanes((64, 128))
    for j in range(BRICKS):
        block = rep_in[(owner_of[j] - at.y + NY) % NY].astype(F32)
        other = pltpu.roll(block, 64, 1)
        returned[0:64, j * 128:(j + 1) * 128] = jnp.where(low_rows, block, other).astype(BF16)
        returned[64:128, j * 128:(j + 1) * 128] = jnp.where(low_rows, other, block).astype(BF16)
    whole = returned[...].astype(F32)
    low_half = low_lanes((COARSE, 512))
    ret_half[:COARSE] = jnp.where(low_half, whole, 0.0).astype(BF16)
    ret_half[COARSE:] = jnp.where(low_half, 0.0, whole).astype(BF16)
    spread = mul(w_down[...].reshape(8 * FINE, COARSE), returned[...])
    low_half = low_lanes((FINE, 512))
    for pair in range(4):
        even = spread[2 * pair * FINE:(2 * pair + 1) * FINE]
        odd = spread[(2 * pair + 1) * FINE:(2 * pair + 2) * FINE]
        both = jnp.where(low_half, even, odd).astype(BF16)
        for j in range(BRICKS):
            back[j * FINE:(j + 1) * FINE, pair * 128:(pair + 1) * 128] = both[:, j * 128:(j + 1) * 128]
    grad_act = mul(back[...], oct_m[...], NT)
    grad_pre = jnp.where(active[...].astype(F32) > 0, grad_act, 0.0)
    for j in range(BRICKS):
        brick = grad_pre[j * FINE:(j + 1) * FINE]
        sides = turned(brick) + [jnp.zeros((FINE, 128), F32)]
        for i in range(5):
            lanes = slice(j * PLANES + i * 128, j * PLANES + (i + 1) * 128)
            middle = brick[:, i * 128:(i + 1) * 128] if i < 4 else sides[4]
            shifted[0:FINE, lanes] = jnp.where(low, sides[i], sides[(i + 1) % 5]).astype(BF16)
            shifted[FINE:2 * FINE, lanes] = middle.astype(BF16)
            shifted[2 * FINE:, lanes] = jnp.where(low, sides[i - 1], sides[i]).astype(BF16)

    part = mul(shifted[...], window[...], NT)
    for b in range(SUB_BLOCKS):
        width = min(128, TAPS * FINE - b * 128)
        first_sum.grads[b * SUB_ROWS:(b + 1) * SUB_ROWS, 0:width] = part[:, b * 128:b * 128 + width]
    first = first_sum.phases()
    next(first)
    part = mul(act_oct[...], ret_half[...], NT)
    for parity in range(2):
        last_sum.grads[parity * DOWN_ROWS:(parity + 1) * DOWN_ROWS] = part[:, parity * 128:(parity + 1) * 128]
    last = last_sum.phases()
    next(last)

    def place_octants():
        for k in range(1, NY):
            link(15 + k, oct_out.at[k], oct_in.at[k], at.along_y(-k)).wait_recv()
        for slot in range(16):
            s, m = slot // 8, slot % 8
            block = chosen(lab_in[0], slot, oct_in[0])
            for k in range(1, NY):
                block = block + chosen(lab_in[k], slot, oct_in[k])
            block = block.astype(F32)
            lanes = slice(m * 128, (m + 1) * 128)
            place_in[s * 128:s * 128 + 64, lanes] = jnp.where(low_rows, block, 0.0).astype(BF16)
            place_in[s * 128 + 64:s * 128 + 128, lanes] = jnp.where(low_rows, 0.0, block).astype(BF16)
        result = mul(place_in[...], place_m[...]).astype(BF16)
        for s in range(2):
            coarse[s] = result[s * COARSE:(s + 1) * COARSE]

    save = pltpu.make_async_copy(coarse, out_coarse, load_sem.at[len(loads)])
    for chunk in (first, last, first, last):
        next(chunk)
    place_octants()
    save.start()
    for chunk in (first, last, first, last, last, first, first, last, first, last):
        next(chunk)
    for copy in started:
        copy.wait_send()
    first_sum.finish()
    last_sum.finish()
    save.wait()


def unpack_kernel(first, last, coarse_in, coarse, grad_sub, grad_down, sub, down, sems):
    copies = [pltpu.make_async_copy(coarse_in, coarse, sems.at[0])]
    copies[0].start()
    for octant in range(8):
        row = octant % 2 * DOWN_ROWS + octant // 2 * FINE
        down[octant] = last[row:row + FINE].astype(F32)
    copies.append(pltpu.make_async_copy(down, grad_down, sems.at[1]))
    copies[-1].start()

    def block(b, kx):
        row = b * SUB_ROWS + kx * FINE
        return first[row:row + FINE].astype(F32)

    lane = lax.broadcasted_iota(jnp.int32, (FINE, 128), 1)
    for kx in range(3):
        for t in range(TAPS):
            b, offset = t * FINE // 128, t * FINE % 128
            left = block(b, kx)
            if offset:
                left = pltpu.roll(left, 128 - offset, 1)
            if offset > 32:
                right = pltpu.roll(block(b + 1, kx), 128 - offset, 1)
                left = jnp.where(lane < 128 - offset, left, right)
            sub[TAPS * kx + t] = left[:, :FINE]
        taps = pl.ds(TAPS * kx, TAPS)
        copies.append(pltpu.make_async_copy(sub.at[taps], grad_sub.at[taps], sems.at[2 + kx]))
        copies[-1].start()
    for copy in copies:
        copy.wait()


def per_device(sizes, features, occupancy, neighbours, owners, octslots, cotangent, w_sub, w_down):
    vmem = pl.BlockSpec(memory_space=pltpu.VMEM)
    smem = pl.BlockSpec(memory_space=pltpu.SMEM)
    hbm = pl.BlockSpec(memory_space=pl.ANY)
    v = pltpu.VMEM
    held = [features[0], occupancy[0], jnp.asarray(padding_matrix()), jnp.asarray(tap_matrix()),
            cotangent[0], jnp.asarray(placing_matrix()), w_sub, jnp.transpose(w_down, (0, 2, 1)),
            jnp.asarray(octant_matrix())]
    rows = [sum_rows(sizes, piece) for piece in (FIRST_PIECE, LAST_PIECE)]
    first, last, coarse = pl.pallas_call(
        functools.partial(kernel, sizes),
        out_shape=(
            jax.ShapeDtypeStruct((rows[0], 128), BF16),
            jax.ShapeDtypeStruct((rows[1], 128), BF16),
            jax.ShapeDtypeStruct(cotangent.shape[1:], BF16),
        ),
        in_specs=[smem] * 3 + [hbm] * 9,
        out_specs=(hbm, hbm, hbm),
        scratch_shapes=[v(a.shape, a.dtype) for a in held] + [
            pltpu.SemaphoreType.DMA((10,)),
            v((BRICKS + 1, FINE, 512), BF16),
            v((BRICKS + 1, FINE, 128), BF16),
            v((BRICKS + 1, FINE, 128), BF16),
            v((BRICKS * 4 * FINE, TAPS * 128), BF16),
            v((BRICKS * FINE, TAPS * 128), BF16),
            v((TAPS * FINE, BRICKS * PLANES), BF16),
            v((BRICKS * FINE, 512), BF16),
            v((4 * FINE, BRICKS * 128), BF16),
            v((3 * FINE, TAPS * FINE), BF16),
            v((4 * FINE, 2 * COARSE), BF16),
            v((BRICKS + 1, 64, 128), BF16),
            v((NY, 64, 128), BF16),
            v((NY, 64, 128), BF16),
            v((NY, 8, 128), jnp.int32),
            v((NY, 8, 128), jnp.int32),
            v((16, 64, 128), BF16),
            v((NY, 64, 128), BF16),
            v((NY, 64, 128), BF16),
            v((COARSE, BRICKS * 128), BF16),
            v((2 * COARSE, BRICKS * 128), BF16),
            v((BRICKS * FINE, 512), BF16),
            v((3 * FINE, BRICKS * PLANES), BF16),
            v((2 * COARSE, 1024), BF16),
            v((2, COARSE, 512), BF16),
            pltpu.SemaphoreType.DMA((2 + 3 * (NY - 1),)),
            pltpu.SemaphoreType.DMA((2 + 3 * (NY - 1),)),
        ] + sum_scratch(sizes, FIRST_PIECE, FIRST_ORDER) + sum_scratch(sizes, LAST_PIECE, LAST_ORDER),
        compiler_params=pltpu.CompilerParams(
            collective_id=0, has_side_effects=True, vmem_limit_bytes=56 * 2**20
        ),
    )(neighbours[0], owners[0], octslots[0], *held)
    coarse, grad_sub, grad_down = pl.pallas_call(
        unpack_kernel,
        out_shape=(
            jax.ShapeDtypeStruct(cotangent.shape[1:], BF16),
            jax.ShapeDtypeStruct(w_sub.shape, F32),
            jax.ShapeDtypeStruct((8, FINE, COARSE), F32),
        ),
        in_specs=[vmem, vmem, vmem],
        out_specs=(hbm, hbm, hbm),
        scratch_shapes=[
            v(w_sub.shape, F32),
            v((8, FINE, COARSE), F32),
            pltpu.SemaphoreType.DMA((5,)),
        ],
        compiler_params=pltpu.CompilerParams(vmem_limit_bytes=56 * 2**20),
    )(first, last, coarse)
    return coarse[None], grad_sub, jnp.transpose(grad_down, (0, 2, 1))


def solution(mesh):
    sizes = (mesh.shape["space"] // NY, mesh.shape["rep"] // 2)
    return jax.shard_map(
        functools.partial(per_device, sizes),
        mesh=mesh,
        in_specs=(
            P("rep", "space", None, None),
            P("rep", "space", None),
            P("rep", "space", None),
            P("rep", "space"),
            P("rep", "space"),
            P("rep", "space", None, None),
            P(),
            P(),
        ),
        out_specs=(P("rep", "space", None, None), P(), P()),
        check_vma=False,
    )
```

```python
import functools

import jax
import jax.numpy as jnp
import numpy as np
from jax import lax
from jax.experimental import pallas as pl
from jax.experimental.pallas import tpu as pltpu
from jax.sharding import PartitionSpec as P

MESH = pl.DeviceIdType.MESH
F32, BF16 = jnp.float32, jnp.bfloat16
NT = (((1,), (1,)), ((), ()))
NN = (((1,), (0,)), ((), ()))
TN = (((0,), (0,)), ((), ()))
NY = 8
BRICKS = 4
FINE = 96
COARSE = 128
TAPS = 9
PLANES = 640
SUB_ROWS = 3 * FINE
DOWN_ROWS = 4 * FINE
SUB_BLOCKS = 7
PIECE = 48
SHARE = NY * PIECE
DOWN_START = SUB_BLOCKS * SUB_ROWS
USED_ROWS = DOWN_START + 2 * DOWN_ROWS


class Place:
    def __init__(self, sizes):
        self.nz, self.nx = sizes
        space, rep = lax.axis_index("space"), lax.axis_index("rep")
        self.z, self.y = space // NY, space % NY
        self.x, self.core = rep // 2, rep % 2

    def across(self):
        return (self.z * NY + self.y, self.x * 2 + 1 - self.core)

    def along_y(self, k):
        return (self.z * NY + (self.y + k) % NY, self.x * 2 + self.core)

    def along_z(self, k):
        return ((self.z + k) % self.nz * NY + self.y, self.x * 2 + self.core)

    def in_plane(self, i, k):
        y = (self.y + k * (1 - self.core)) % NY
        z = (self.z + k * self.core) % NY
        return (z * NY + y, (self.x + i) % self.nx * 2 + self.core)

    def across_planes(self, k):
        y = (self.y + k * self.core) % NY
        z = (self.z + k * (1 - self.core)) % NY
        return (z * NY + y, self.x * 2 + self.core)

    def sum_partners(self):
        far = [self.along_y(k) for k in far_first(NY)]
        far += [self.in_plane(i, k) for i in far_first(self.nx) for k in far_first(NY) + [0]]
        far += [self.along_z(k) for k in far_first(NY)]
        return far + [self.across()]


def rows_at(start, count):
    return pl.ds(pl.multiple_of(start, 16), count)


def near_first(count):
    return sorted(range(1, count), key=lambda k: min(k, count - k))


def far_first(count):
    return near_first(count)[::-1]


def sum_scratch(nx):
    half = nx * SHARE
    copies = 2 * nx + 2 * nx * NY + NY
    return [
        pltpu.VMEM((2 * half, 128), F32),
        pltpu.VMEM((half, 128), BF16),
        pltpu.VMEM((half, 128), BF16),
        pltpu.VMEM((nx, SHARE, 128), BF16),
        pltpu.VMEM((nx * NY, PIECE, 128), BF16),
        pltpu.VMEM((SHARE, 128), F32),
        pltpu.VMEM((NY, PIECE, 128), BF16),
        pltpu.VMEM((2 * half, 128), BF16),
        pltpu.SemaphoreType.DMA((copies,)),
        pltpu.SemaphoreType.DMA((copies,)),
        pltpu.SemaphoreType.DMA((2 * nx,)),
    ]


class GradSum:
    def __init__(self, place, scratch, result):
        self.place, self.result = place, result
        (self.grads, self.core_out, self.core_in, self.plane_out, self.plane_in, self.mine,
         self.across_all, self.total, self.send_sem, self.recv_sem, self.save_sem) = scratch
        self.used = 0
        self.sent = []
        self.saved = []

    def slots(self, count):
        self.used += count
        return range(self.used - count, self.used)

    def send(self, slot, src, dst, device):
        copy = pltpu.make_async_remote_copy(
            src_ref=src, dst_ref=dst, send_sem=self.send_sem.at[slot],
            recv_sem=self.recv_sem.at[slot], device_id=device, device_id_type=MESH)
        copy.start()
        self.sent.append(copy)

    def arrive(self, slot, dst, device):
        pltpu.make_async_remote_copy(
            src_ref=dst, dst_ref=dst, send_sem=self.send_sem.at[slot],
            recv_sem=self.recv_sem.at[slot], device_id=device, device_id_type=MESH).wait_recv()

    def save(self, rows):
        save = pltpu.make_async_copy(
            self.total.at[rows], self.result.at[rows], self.save_sem.at[len(self.saved)])
        save.start()
        self.saved.append(save)

    def start(self):
        at, grads = self.place, self.grads
        half = at.nx * SHARE
        self.core_slots = self.slots(at.nx)
        self.far_x = far_first(at.nx) + [0]
        self.near_x = self.far_x[::-1]
        for i in self.far_x:
            rows = self.share(i)
            start = (1 - at.core) * half + (at.x + i) % at.nx * SHARE
            self.core_out[rows] = grads[rows_at(start, SHARE)].astype(BF16)
            self.send(self.core_slots[i], self.core_out.at[rows], self.core_in.at[rows], at.across())

    def share(self, i):
        return rows_at((self.place.x + i) % self.place.nx * SHARE, SHARE)

    def run(self, meanwhile):
        at, grads, nx = self.place, self.grads, self.place.nx
        half = nx * SHARE
        core = at.core
        b = core * at.z + (1 - core) * at.y
        c = core * at.y + (1 - core) * at.z
        far, near = far_first(NY) + [0], [0] + near_first(NY)
        slots = self.slots(nx * NY)
        for i in self.far_x:
            rows = self.share(i)
            self.arrive(self.core_slots[i], self.core_in.at[rows], at.across())
            start = core * half + (at.x + i) % nx * SHARE
            pair = grads[rows_at(start, SHARE)] + self.core_in[rows].astype(F32)
            self.plane_out[i] = pair.astype(BF16)
            if i == 0:
                self.mine[...] = pair
            for k in far:
                if i or k:
                    self.send(slots[i * NY + k],
                              self.plane_out.at[i, rows_at((b + k) % NY * PIECE, PIECE)],
                              self.plane_in.at[i * NY + k], at.in_plane(i, k))
        meanwhile()
        summed = self.mine[rows_at(b * PIECE, PIECE)]
        for i in self.near_x:
            for k in near:
                if i or k:
                    slot = i * NY + k
                    self.arrive(slots[slot], self.plane_in.at[slot], at.in_plane(-i, -k))
                    summed = summed + self.plane_in[slot].astype(F32)
        self.across_all[c] = summed.astype(BF16)
        slots = self.slots(NY)
        for k in far_first(NY):
            self.send(slots[k], self.across_all.at[c], self.across_all.at[c], at.across_planes(k))
        for k in near_first(NY):
            self.arrive(slots[k], self.across_all.at[(c - k) % NY], at.across_planes(-k))
        summed = self.across_all[0].astype(F32)
        for layer in range(1, NY):
            summed = summed + self.across_all[layer].astype(F32)

        def share_of(which, i):
            return rows_at(which * half + (at.x + i) % nx * SHARE, SHARE)

        def piece_of(i, k):
            start = core * half + (at.x + i) % nx * SHARE + (b + k) % NY * PIECE
            return self.total.at[rows_at(start, PIECE)]

        self.total[rows_at(core * half + at.x * SHARE + b * PIECE, PIECE)] = summed.astype(BF16)
        slots = self.slots(nx * NY)
        for i in self.far_x:
            for k in far:
                if i or k:
                    self.send(slots[i * NY + k], piece_of(0, 0), piece_of(0, 0), at.in_plane(i, k))
        core_slots = self.slots(nx)
        for i in self.near_x:
            for k in near:
                if i or k:
                    self.arrive(slots[i * NY + k], piece_of(-i, -k), at.in_plane(-i, -k))
            other = self.total.at[share_of(core, -i)]
            self.send(core_slots[i], other, other, at.across())
            self.save(share_of(core, -i))
        for i in self.near_x:
            self.arrive(core_slots[i], self.total.at[share_of(1 - core, -i)], at.across())
            self.save(share_of(1 - core, -i))

    def finish(self):
        for copy in self.sent:
            copy.wait_send()
        for save in self.saved:
            save.wait()


def mul(a, b, dims=NN):
    return lax.dot_general(a, b, dims, preferred_element_type=F32)


def padding_matrix():
    out = np.zeros((9, 2, 8, 8, 2, 128), np.float32)
    sides = ([(7, 0)], [(i, i + 1) for i in range(8)], [(0, 9)])
    for layer_y in range(3):
        for layer_z in range(3):
            for y, to_y in sides[layer_y]:
                for z, to_z in sides[layer_z]:
                    for half in range(2):
                        out[3 * layer_y + layer_z, half, y, z, half, 10 * to_y + to_z] = 1
    return out.reshape(9 * 128, 256).astype(jnp.bfloat16)


def tap_matrix():
    out = np.zeros((2, 128, 9, 2, 8, 8), np.float32)
    for tap in range(9):
        for y in range(8):
            for z in range(8):
                for half in range(2):
                    out[half, 10 * (y + tap // 3) + z + tap % 3, tap, half, y, z] = 1
    return out.reshape(256, 9 * 128).astype(jnp.bfloat16)


def octant_matrix():
    out = np.zeros((8, 8, 8, 8, 64), np.float32)
    for x in range(8):
        for y in range(8):
            for z in range(8):
                octant = x % 2 * 4 + y % 2 * 2 + z % 2
                out[x, y, z, octant, x // 2 * 16 + y // 2 * 4 + z // 2] = 1
    return out.reshape(512, 512).astype(jnp.bfloat16)


def placing_matrix():
    out = np.zeros((8, 2, 64, 8, 8, 8), np.float32)
    for octant in range(8):
        for v in range(64):
            x, y, z = v // 16, v // 4 % 4, v % 4
            spot = (octant // 4 * 4 + x, octant // 2 % 2 * 4 + y, octant % 2 * 4 + z)
            out[(octant, slice(None), v) + spot] = 1
    return out.reshape(1024, 512).astype(jnp.bfloat16)


def low_lanes(shape):
    return lax.broadcasted_iota(jnp.int32, shape, len(shape) - 1) % 128 < 64


def packed(block):
    return jnp.where(low_lanes((64, 128)), block[:64], block[64:])


def chosen(labels, slot, table):
    hit = jnp.where(labels[0:1] == slot, 1.0, 0.0).astype(BF16)
    return hit * table


def kernel(sizes, neighbours, owners, octslots, *refs):
    held, (out_total, out_coarse) = refs[:9], refs[9:11]
    loaded, refs = refs[11:20], refs[20:]
    features, occupancy, pad_m, tap_m, cotangent, place_m, w_sub, w_down, oct_m = loaded
    (load_sem, source, upper, lower, gathered, edge, window, active, act_oct, w_cat, w_pair,
     oct_pack, oct_out, oct_in, lab_out, lab_in, table, rep_out, rep_in, returned, ret_half,
     back, shifted, place_in, coarse, pair_send, pair_recv) = refs[:27]
    at = Place(sizes)
    work = GradSum(at, refs[27:], out_total)
    grads = work.grads
    nspace = at.nz * NY
    me = at.z * NY + at.y
    rep = at.x * 2 + at.core
    above, below = ((me + 1) % nspace, rep), ((me + nspace - 1) % nspace, rep)
    partners = at.sum_partners() + [above, below]
    barrier = pltpu.get_barrier_semaphore()
    for partner in partners:
        pl.semaphore_signal(barrier, inc=1, device_id=partner, device_id_type=MESH)
    loads = [pltpu.make_async_copy(src, dst, load_sem.at[i])
             for i, (src, dst) in enumerate(zip(held, loaded))]
    for load in loads:
        load.start()

    def link(slot, src, dst, device):
        return pltpu.make_async_remote_copy(
            src_ref=src, dst_ref=dst, send_sem=pair_send.at[slot], recv_sem=pair_recv.at[slot],
            device_id=device, device_id_type=MESH)

    started = []

    def send(slot, src, dst, device):
        copy = link(slot, src, dst, device)
        copy.start()
        started.append(copy)

    for load in loads[:2]:
        load.wait()
    occ = occupancy[...].astype(BF16)
    for j in range(BRICKS):
        source[j] = features[j] * occ[j:j + 1]
    source[BRICKS] = jnp.zeros((FINE, 512), BF16)
    upper[BRICKS] = jnp.zeros((FINE, 128), BF16)
    lower[BRICKS] = jnp.zeros((FINE, 128), BF16)
    owner_of = [owners[j] % NY for j in range(BRICKS)]

    def brick_for(member):
        found = BRICKS
        for j in range(BRICKS):
            found = jnp.where(owner_of[j] == member, j, found)
        return found

    for k in range(NY):
        member = (at.y + k) % NY
        label = -1
        for j in range(BRICKS):
            label = jnp.where(owner_of[j] == member, octslots[j], label)
        lab_out[k] = jnp.full((8, 128), label, jnp.int32)

    grads[(SUB_BLOCKS - 1) * SUB_ROWS:DOWN_START] = jnp.zeros((SUB_ROWS, 128), F32)
    grads[USED_ROWS:] = jnp.zeros((grads.shape[0] - USED_ROWS, 128), F32)

    def own_planes(bricks):
        for j in bricks:
            for n in range(9):
                which = jnp.clip(neighbours[j, 9 + n] - BRICKS, 0, BRICKS)
                for p in range(4):
                    row = (j * 4 + p) * FINE
                    gathered[row:row + FINE, n * 128:(n + 1) * 128] = (
                        source[which, :, p * 128:(p + 1) * 128])
        start = bricks[0] * 4 * FINE
        planes = mul(gathered[start:start + len(bricks) * 4 * FINE], pad_m[...]).astype(BF16)
        planes = mul(planes, tap_m[...]).astype(BF16)
        for j in bricks:
            for p in range(4):
                row, column = (j * 4 + p) * FINE - start, j * PLANES + p * 128
                for t in range(TAPS):
                    window[t * FINE:(t + 1) * FINE, column:column + 128] = (
                        planes[row:row + FINE, t * 128:(t + 1) * 128])

    for load in loads[2:4]:
        load.wait()
    own_planes(range(2))
    pl.semaphore_wait(barrier, len(partners))
    own, head, tail = pl.ds(0, BRICKS), pl.ds(0, 128), pl.ds(384, 128)
    for k in far_first(NY):
        send(1 + k, lab_out.at[k], lab_in.at[k], at.along_y(k))
    send(0, source.at[own, :, tail], lower.at[own], above)
    send(1, source.at[own, :, head], upper.at[own], below)
    lab_in[0] = lab_out[0]

    own_planes(range(2, BRICKS))
    for load in loads[4:]:
        load.wait()
    spread = mul(cotangent[...].reshape(2 * COARSE, 512), place_m[...], NT)
    for s in range(2):
        for m in range(8):
            block = spread[s * COARSE:(s + 1) * COARSE, m * 128:(m + 1) * 128]
            table[8 * s + m] = packed(block).astype(BF16)
    for kx in range(3):
        w_cat[kx * FINE:(kx + 1) * FINE] = jnp.concatenate(
            [w_sub[TAPS * kx + t] for t in range(TAPS)], axis=1)
    for pair in range(4):
        for parity in range(2):
            w_pair[pair * FINE:(pair + 1) * FINE, parity * 128:(parity + 1) * 128] = (
                w_down[2 * pair + parity])

    for k in [0] + near_first(NY):
        if k:
            link(1 + k, lab_out.at[k], lab_in.at[k], at.along_y(-k)).wait_recv()
        labels = lab_in[k]
        answer = chosen(labels, 0, table[0])
        for slot in range(1, 16):
            answer = answer + chosen(labels, slot, table[slot])
        if k:
            rep_out[k] = answer
            send(8 + k, rep_out.at[k], rep_in.at[k], at.along_y(-k))
        else:
            rep_in[0] = answer

    link(0, source.at[own, :, tail], lower.at[own], below).wait_recv()
    link(1, source.at[own, :, head], upper.at[own], above).wait_recv()
    low = low_lanes((FINE, 128))
    for j in range(BRICKS):
        for n in range(9):
            which_low = jnp.clip(neighbours[j, n], 0, BRICKS)
            which_high = jnp.clip(neighbours[j, 18 + n] - 2 * BRICKS, 0, BRICKS)
            edge[j * FINE:(j + 1) * FINE, n * 128:(n + 1) * 128] = jnp.where(
                low, upper[which_high], lower[which_low])
    planes = mul(edge[...], pad_m[...]).astype(BF16)
    planes = mul(planes, tap_m[...]).astype(BF16)
    for j in range(BRICKS):
        column = j * PLANES + 512
        for t in range(TAPS):
            window[t * FINE:(t + 1) * FINE, column:column + 128] = (
                planes[j * FINE:(j + 1) * FINE, t * 128:(t + 1) * 128])

    def turned(rows):
        return [pltpu.roll(rows[:, i * 128:(i + 1) * 128], 64, 1) for i in range(rows.shape[1] // 128)]

    for two in range(BRICKS // 2):
        columns = slice(2 * two * PLANES, 2 * (two + 1) * PLANES)
        wide = mul(w_cat[...], window[:, columns])
        for j in (2 * two, 2 * two + 1):
            brick = wide[:, j % 2 * PLANES:(j % 2 + 1) * PLANES]
            behind, ahead = turned(brick[:FINE]), turned(brick[2 * FINE:])
            for i in range(4):
                lanes = slice(i * 128, (i + 1) * 128)
                total = brick[FINE:2 * FINE, lanes]
                total = total + jnp.where(low, ahead[i], ahead[i + 1])
                total = total + jnp.where(low, behind[i - 1], behind[i])
                pre_act = total * occupancy[j:j + 1, lanes].astype(F32)
                active[j * FINE:(j + 1) * FINE, lanes] = jnp.maximum(pre_act, 0.0).astype(BF16)

    octants = mul(active[...], oct_m[...]).astype(BF16)
    for j in range(BRICKS):
        for pair in range(4):
            act_oct[pair * FINE:(pair + 1) * FINE, j * 128:(j + 1) * 128] = (
                octants[j * FINE:(j + 1) * FINE, pair * 128:(pair + 1) * 128])
    summed = mul(w_pair[...], act_oct[...], TN)
    for j in range(BRICKS):
        even = summed[:COARSE, j * 128:(j + 1) * 128]
        odd = summed[COARSE:, j * 128:(j + 1) * 128]
        both = jnp.where(low_lanes((COARSE, 128)), even, odd)
        both = both + pltpu.roll(both, 64, 1)
        oct_pack[j] = packed(both).astype(BF16)
    oct_pack[BRICKS] = jnp.zeros((64, 128), BF16)
    for k in far_first(NY) + [0]:
        block = oct_pack[brick_for((at.y + k) % NY)]
        if k:
            oct_out[k] = block
            send(15 + k, oct_out.at[k], oct_in.at[k], at.along_y(k))
        else:
            oct_in[0] = block

    for k in range(1, NY):
        link(8 + k, rep_out.at[k], rep_in.at[k], at.along_y(k)).wait_recv()
    low_rows = low_lanes((64, 128))
    for j in range(BRICKS):
        block = rep_in[(owner_of[j] - at.y + NY) % NY].astype(F32)
        other = pltpu.roll(block, 64, 1)
        returned[0:64, j * 128:(j + 1) * 128] = jnp.where(low_rows, block, other).astype(BF16)
        returned[64:128, j * 128:(j + 1) * 128] = jnp.where(low_rows, other, block).astype(BF16)
    whole = returned[...].astype(F32)
    low_half = low_lanes((COARSE, 512))
    ret_half[:COARSE] = jnp.where(low_half, whole, 0.0).astype(BF16)
    ret_half[COARSE:] = jnp.where(low_half, 0.0, whole).astype(BF16)
    spread = mul(w_down[...].reshape(8 * FINE, COARSE), returned[...])
    low_half = low_lanes((FINE, 512))
    for pair in range(4):
        even = spread[2 * pair * FINE:(2 * pair + 1) * FINE]
        odd = spread[(2 * pair + 1) * FINE:(2 * pair + 2) * FINE]
        both = jnp.where(low_half, even, odd).astype(BF16)
        for j in range(BRICKS):
            back[j * FINE:(j + 1) * FINE, pair * 128:(pair + 1) * 128] = both[:, j * 128:(j + 1) * 128]
    grad_act = mul(back[...], oct_m[...], NT)
    grad_pre = jnp.where(active[...].astype(F32) > 0, grad_act, 0.0)
    for j in range(BRICKS):
        brick = grad_pre[j * FINE:(j + 1) * FINE]
        sides = turned(brick) + [jnp.zeros((FINE, 128), F32)]
        for i in range(5):
            lanes = slice(j * PLANES + i * 128, j * PLANES + (i + 1) * 128)
            middle = brick[:, i * 128:(i + 1) * 128] if i < 4 else sides[4]
            shifted[0:FINE, lanes] = jnp.where(low, sides[i], sides[(i + 1) % 5]).astype(BF16)
            shifted[FINE:2 * FINE, lanes] = middle.astype(BF16)
            shifted[2 * FINE:, lanes] = jnp.where(low, sides[i - 1], sides[i]).astype(BF16)

    part = mul(act_oct[...], ret_half[...], NT)
    for parity in range(2):
        start = DOWN_START + parity * DOWN_ROWS
        grads[start:start + DOWN_ROWS] = part[:, parity * 128:(parity + 1) * 128]
    part = mul(shifted[...], window[...], NT)
    for b in range(SUB_BLOCKS):
        width = min(128, TAPS * FINE - b * 128)
        grads[b * SUB_ROWS:(b + 1) * SUB_ROWS, 0:width] = part[:, b * 128:b * 128 + width]
    work.start()

    def place_octants():
        for k in range(1, NY):
            link(15 + k, oct_out.at[k], oct_in.at[k], at.along_y(-k)).wait_recv()
        for slot in range(16):
            s, m = slot // 8, slot % 8
            block = chosen(lab_in[0], slot, oct_in[0])
            for k in range(1, NY):
                block = block + chosen(lab_in[k], slot, oct_in[k])
            block = block.astype(F32)
            lanes = slice(m * 128, (m + 1) * 128)
            place_in[s * 128:s * 128 + 64, lanes] = jnp.where(low_rows, block, 0.0).astype(BF16)
            place_in[s * 128 + 64:s * 128 + 128, lanes] = jnp.where(low_rows, 0.0, block).astype(BF16)
        result = mul(place_in[...], place_m[...]).astype(BF16)
        for s in range(2):
            coarse[s] = result[s * COARSE:(s + 1) * COARSE]

    save = pltpu.make_async_copy(coarse, out_coarse, load_sem.at[len(loads)])
    def while_waiting():
        place_octants()
        save.start()

    work.run(while_waiting)
    for copy in started:
        copy.wait_send()
    work.finish()
    save.wait()


def unpack_kernel(total, coarse_in, coarse, grad_sub, grad_down, sub, down, sems):
    copies = [pltpu.make_async_copy(coarse_in, coarse, sems.at[0])]
    copies[0].start()
    for octant in range(8):
        row = DOWN_START + octant % 2 * DOWN_ROWS + octant // 2 * FINE
        down[octant] = total[row:row + FINE].astype(F32)
    copies.append(pltpu.make_async_copy(down, grad_down, sems.at[1]))
    copies[-1].start()

    def block(b, kx):
        row = b * SUB_ROWS + kx * FINE
        return total[row:row + FINE].astype(F32)

    lane = lax.broadcasted_iota(jnp.int32, (FINE, 128), 1)
    for kx in range(3):
        for t in range(TAPS):
            b, offset = t * FINE // 128, t * FINE % 128
            left = block(b, kx)
            if offset:
                left = pltpu.roll(left, 128 - offset, 1)
            if offset > 32:
                right = pltpu.roll(block(b + 1, kx), 128 - offset, 1)
                left = jnp.where(lane < 128 - offset, left, right)
            sub[TAPS * kx + t] = left[:, :FINE]
        taps = pl.ds(TAPS * kx, TAPS)
        copies.append(pltpu.make_async_copy(sub.at[taps], grad_sub.at[taps], sems.at[2 + kx]))
        copies[-1].start()
    for copy in copies:
        copy.wait()


def per_device(sizes, features, occupancy, neighbours, owners, octslots, cotangent, w_sub, w_down):
    vmem = pl.BlockSpec(memory_space=pltpu.VMEM)
    smem = pl.BlockSpec(memory_space=pltpu.SMEM)
    hbm = pl.BlockSpec(memory_space=pl.ANY)
    v = pltpu.VMEM
    held = [features[0], occupancy[0], jnp.asarray(padding_matrix()), jnp.asarray(tap_matrix()),
            cotangent[0], jnp.asarray(placing_matrix()), w_sub, jnp.transpose(w_down, (0, 2, 1)),
            jnp.asarray(octant_matrix())]
    total, coarse = pl.pallas_call(
        functools.partial(kernel, sizes),
        out_shape=(
            jax.ShapeDtypeStruct((2 * sizes[1] * SHARE, 128), BF16),
            jax.ShapeDtypeStruct(cotangent.shape[1:], BF16),
        ),
        in_specs=[smem] * 3 + [hbm] * 9,
        out_specs=(hbm, hbm),
        scratch_shapes=[v(a.shape, a.dtype) for a in held] + [
            pltpu.SemaphoreType.DMA((10,)),
            v((BRICKS + 1, FINE, 512), BF16),
            v((BRICKS + 1, FINE, 128), BF16),
            v((BRICKS + 1, FINE, 128), BF16),
            v((BRICKS * 4 * FINE, TAPS * 128), BF16),
            v((BRICKS * FINE, TAPS * 128), BF16),
            v((TAPS * FINE, BRICKS * PLANES), BF16),
            v((BRICKS * FINE, 512), BF16),
            v((4 * FINE, BRICKS * 128), BF16),
            v((3 * FINE, TAPS * FINE), BF16),
            v((4 * FINE, 2 * COARSE), BF16),
            v((BRICKS + 1, 64, 128), BF16),
            v((NY, 64, 128), BF16),
            v((NY, 64, 128), BF16),
            v((NY, 8, 128), jnp.int32),
            v((NY, 8, 128), jnp.int32),
            v((16, 64, 128), BF16),
            v((NY, 64, 128), BF16),
            v((NY, 64, 128), BF16),
            v((COARSE, BRICKS * 128), BF16),
            v((2 * COARSE, BRICKS * 128), BF16),
            v((BRICKS * FINE, 512), BF16),
            v((3 * FINE, BRICKS * PLANES), BF16),
            v((2 * COARSE, 1024), BF16),
            v((2, COARSE, 512), BF16),
            pltpu.SemaphoreType.DMA((2 + 3 * (NY - 1),)),
            pltpu.SemaphoreType.DMA((2 + 3 * (NY - 1),)),
        ] + sum_scratch(sizes[1]),
        compiler_params=pltpu.CompilerParams(
            collective_id=0, has_side_effects=True, vmem_limit_bytes=56 * 2**20
        ),
    )(neighbours[0], owners[0], octslots[0], *held)
    coarse, grad_sub, grad_down = pl.pallas_call(
        unpack_kernel,
        out_shape=(
            jax.ShapeDtypeStruct(cotangent.shape[1:], BF16),
            jax.ShapeDtypeStruct(w_sub.shape, F32),
            jax.ShapeDtypeStruct((8, FINE, COARSE), F32),
        ),
        in_specs=[vmem, vmem],
        out_specs=(hbm, hbm, hbm),
        scratch_shapes=[
            v(w_sub.shape, F32),
            v((8, FINE, COARSE), F32),
            pltpu.SemaphoreType.DMA((5,)),
        ],
        compiler_params=pltpu.CompilerParams(vmem_limit_bytes=56 * 2**20),
    )(total, coarse)
    return coarse[None], grad_sub, jnp.transpose(grad_down, (0, 2, 1))


def solution(mesh):
    sizes = (mesh.shape["space"] // NY, mesh.shape["rep"] // 2)
    return jax.shard_map(
        functools.partial(per_device, sizes),
        mesh=mesh,
        in_specs=(
            P("rep", "space", None, None),
            P("rep", "space", None),
            P("rep", "space", None),
            P("rep", "space"),
            P("rep", "space"),
            P("rep", "space", None, None),
            P(),
            P(),
        ),
        out_specs=(P("rep", "space", None, None), P(), P()),
        check_vma=False,
    )
```

```python
import functools

import jax
import jax.numpy as jnp
import numpy as np
from jax import lax
from jax.experimental import pallas as pl
from jax.experimental.pallas import tpu as pltpu
from jax.sharding import PartitionSpec as P

MESH = pl.DeviceIdType.MESH
F32, BF16 = jnp.float32, jnp.bfloat16
NT = (((1,), (1,)), ((), ()))
NN = (((1,), (0,)), ((), ()))
TN = (((0,), (0,)), ((), ()))
NY = 8
BRICKS = 4
FINE = 96
COARSE = 128
TAPS = 9
PLANES = 640
SUB_ROWS = 3 * FINE
DOWN_ROWS = 4 * FINE
SUB_BLOCKS = 7
PIECE = 48
SHARE = NY * PIECE
DOWN_START = SUB_BLOCKS * SUB_ROWS
USED_ROWS = DOWN_START + 2 * DOWN_ROWS


class Place:
    def __init__(self, sizes):
        self.nz, self.nx = sizes
        space, rep = lax.axis_index("space"), lax.axis_index("rep")
        self.z, self.y = space // NY, space % NY
        self.x, self.core = rep // 2, rep % 2

    def across(self):
        return (self.z * NY + self.y, self.x * 2 + 1 - self.core)

    def along_y(self, k):
        return (self.z * NY + (self.y + k) % NY, self.x * 2 + self.core)

    def along_z(self, k):
        return ((self.z + k) % self.nz * NY + self.y, self.x * 2 + self.core)

    def in_plane(self, i, k):
        y = (self.y + k * (1 - self.core)) % NY
        z = (self.z + k * self.core) % NY
        return (z * NY + y, (self.x + i) % self.nx * 2 + self.core)

    def across_planes(self, k):
        y = (self.y + k * self.core) % NY
        z = (self.z + k * (1 - self.core)) % NY
        return (z * NY + y, self.x * 2 + self.core)

    def sum_partners(self):
        far = [self.along_y(k) for k in far_first(NY)]
        far += [self.in_plane(i, k) for i in far_first(self.nx) for k in far_first(NY) + [0]]
        far += [self.along_z(k) for k in far_first(NY)]
        return far + [self.across()]


def rows_at(start, count):
    return pl.ds(pl.multiple_of(start, 16), count)


def near_first(count):
    return sorted(range(1, count), key=lambda k: min(k, count - k))


def far_first(count):
    return near_first(count)[::-1]


def sum_scratch(nx):
    half = nx * SHARE
    copies = 2 * nx + 2 * nx * NY + NY
    return [
        pltpu.VMEM((2 * half, 128), F32),
        pltpu.VMEM((half, 128), BF16),
        pltpu.VMEM((half, 128), BF16),
        pltpu.VMEM((nx, SHARE, 128), BF16),
        pltpu.VMEM((nx * NY, PIECE, 128), BF16),
        pltpu.VMEM((SHARE, 128), F32),
        pltpu.VMEM((NY, PIECE, 128), BF16),
        pltpu.VMEM((2 * half, 128), BF16),
        pltpu.SemaphoreType.DMA((copies,)),
        pltpu.SemaphoreType.DMA((copies,)),
        pltpu.SemaphoreType.DMA((2 * nx,)),
    ]


class GradSum:
    def __init__(self, place, scratch, result):
        self.place, self.result = place, result
        (self.grads, self.core_out, self.core_in, self.plane_out, self.plane_in, self.mine,
         self.across_all, self.total, self.send_sem, self.recv_sem, self.save_sem) = scratch
        self.used = 0
        self.sent = []
        self.saved = []

    def slots(self, count):
        self.used += count
        return range(self.used - count, self.used)

    def send(self, slot, src, dst, device):
        copy = pltpu.make_async_remote_copy(
            src_ref=src, dst_ref=dst, send_sem=self.send_sem.at[slot],
            recv_sem=self.recv_sem.at[slot], device_id=device, device_id_type=MESH)
        copy.start()
        self.sent.append(copy)

    def arrive(self, slot, dst, device):
        pltpu.make_async_remote_copy(
            src_ref=dst, dst_ref=dst, send_sem=self.send_sem.at[slot],
            recv_sem=self.recv_sem.at[slot], device_id=device, device_id_type=MESH).wait_recv()

    def save(self, rows):
        save = pltpu.make_async_copy(
            self.total.at[rows], self.result.at[rows], self.save_sem.at[len(self.saved)])
        save.start()
        self.saved.append(save)

    def start(self):
        at, grads = self.place, self.grads
        half = at.nx * SHARE
        self.core_slots = self.slots(at.nx)
        self.far_x = far_first(at.nx) + [0]
        self.near_x = self.far_x[::-1]
        for i in self.far_x:
            rows = self.share(i)
            start = (1 - at.core) * half + (at.x + i) % at.nx * SHARE
            self.core_out[rows] = grads[rows_at(start, SHARE)].astype(BF16)
            self.send(self.core_slots[i], self.core_out.at[rows], self.core_in.at[rows], at.across())

    def share(self, i):
        return rows_at((self.place.x + i) % self.place.nx * SHARE, SHARE)

    def run(self, meanwhile):
        at, grads, nx = self.place, self.grads, self.place.nx
        half = nx * SHARE
        core = at.core
        b = core * at.z + (1 - core) * at.y
        c = core * at.y + (1 - core) * at.z
        far, near = far_first(NY) + [0], [0] + near_first(NY)
        slots = self.slots(nx * NY)
        for i in self.far_x:
            rows = self.share(i)
            self.arrive(self.core_slots[i], self.core_in.at[rows], at.across())
            start = core * half + (at.x + i) % nx * SHARE
            pair = grads[rows_at(start, SHARE)] + self.core_in[rows].astype(F32)
            self.plane_out[i] = pair.astype(BF16)
            if i == 0:
                self.mine[...] = pair
            for k in far:
                if i or k:
                    self.send(slots[i * NY + k],
                              self.plane_out.at[i, rows_at((b + k) % NY * PIECE, PIECE)],
                              self.plane_in.at[i * NY + k], at.in_plane(i, k))
        meanwhile()
        summed = self.mine[rows_at(b * PIECE, PIECE)]
        for i in self.near_x:
            for k in near:
                if i or k:
                    slot = i * NY + k
                    self.arrive(slots[slot], self.plane_in.at[slot], at.in_plane(-i, -k))
                    summed = summed + self.plane_in[slot].astype(F32)
        self.across_all[c] = summed.astype(BF16)
        older = list(self.sent)
        slots = self.slots(NY)
        for k in far_first(NY):
            self.send(slots[k], self.across_all.at[c], self.across_all.at[c], at.across_planes(k))
        self.settle(older)
        for k in near_first(NY):
            self.arrive(slots[k], self.across_all.at[(c - k) % NY], at.across_planes(-k))
        summed = self.across_all[0].astype(F32)
        for layer in range(1, NY):
            summed = summed + self.across_all[layer].astype(F32)

        def share_of(which, i):
            return rows_at(which * half + (at.x + i) % nx * SHARE, SHARE)

        def piece_of(i, k):
            start = core * half + (at.x + i) % nx * SHARE + (b + k) % NY * PIECE
            return self.total.at[rows_at(start, PIECE)]

        self.total[rows_at(core * half + at.x * SHARE + b * PIECE, PIECE)] = summed.astype(BF16)
        older = list(self.sent)
        slots = self.slots(nx * NY)
        for i in self.far_x:
            for k in far:
                if i or k:
                    self.send(slots[i * NY + k], piece_of(0, 0), piece_of(0, 0), at.in_plane(i, k))
        self.settle(older)
        older = list(self.sent)
        core_slots = self.slots(nx)
        for i in self.near_x:
            for k in near:
                if i or k:
                    self.arrive(slots[i * NY + k], piece_of(-i, -k), at.in_plane(-i, -k))
            other = self.total.at[share_of(core, -i)]
            self.send(core_slots[i], other, other, at.across())
            self.save(share_of(core, -i))
        self.settle(older)
        for i in self.near_x:
            self.arrive(core_slots[i], self.total.at[share_of(1 - core, -i)], at.across())
            self.save(share_of(1 - core, -i))

    def settle(self, copies):
        for copy in copies:
            copy.wait_send()
        self.sent = self.sent[len(copies):]

    def finish(self):
        self.settle(list(self.sent))
        for save in self.saved:
            save.wait()


def mul(a, b, dims=NN):
    return lax.dot_general(a, b, dims, preferred_element_type=F32)


def padding_matrix():
    out = np.zeros((9, 2, 8, 8, 2, 128), np.float32)
    sides = ([(7, 0)], [(i, i + 1) for i in range(8)], [(0, 9)])
    for layer_y in range(3):
        for layer_z in range(3):
            for y, to_y in sides[layer_y]:
                for z, to_z in sides[layer_z]:
                    for half in range(2):
                        out[3 * layer_y + layer_z, half, y, z, half, 10 * to_y + to_z] = 1
    return out.reshape(9 * 128, 256).astype(jnp.bfloat16)


def tap_matrix():
    out = np.zeros((2, 128, 9, 2, 8, 8), np.float32)
    for tap in range(9):
        for y in range(8):
            for z in range(8):
                for half in range(2):
                    out[half, 10 * (y + tap // 3) + z + tap % 3, tap, half, y, z] = 1
    return out.reshape(256, 9 * 128).astype(jnp.bfloat16)


def octant_matrix():
    out = np.zeros((8, 8, 8, 8, 64), np.float32)
    for x in range(8):
        for y in range(8):
            for z in range(8):
                octant = x % 2 * 4 + y % 2 * 2 + z % 2
                out[x, y, z, octant, x // 2 * 16 + y // 2 * 4 + z // 2] = 1
    return out.reshape(512, 512).astype(jnp.bfloat16)


def placing_matrix():
    out = np.zeros((8, 2, 64, 8, 8, 8), np.float32)
    for octant in range(8):
        for v in range(64):
            x, y, z = v // 16, v // 4 % 4, v % 4
            spot = (octant // 4 * 4 + x, octant // 2 % 2 * 4 + y, octant % 2 * 4 + z)
            out[(octant, slice(None), v) + spot] = 1
    return out.reshape(1024, 512).astype(jnp.bfloat16)


def low_lanes(shape):
    return lax.broadcasted_iota(jnp.int32, shape, len(shape) - 1) % 128 < 64


def packed(block):
    return jnp.where(low_lanes((64, 128)), block[:64], block[64:])


def chosen(labels, slot, table):
    hit = jnp.where(labels[0:1] == slot, 1.0, 0.0).astype(BF16)
    return hit * table


def kernel(sizes, *refs):
    held, (out_total, out_coarse) = refs[:12], refs[12:14]
    loaded, refs = refs[14:26], refs[26:]
    neighbours, owners, octslots, features, occupancy, pad_m, tap_m, cotangent, place_m, w_sub, w_down, oct_m = loaded
    (load_sem, source, upper, lower, gathered, edge, window, active, act_oct, w_cat, w_pair,
     oct_pack, oct_out, oct_in, lab_out, lab_in, table, rep_out, rep_in, returned, ret_half,
     back, shifted, place_in, coarse, pair_send, pair_recv) = refs[:27]
    at = Place(sizes)
    work = GradSum(at, refs[27:], out_total)
    grads = work.grads
    nspace = at.nz * NY
    me = at.z * NY + at.y
    rep = at.x * 2 + at.core
    above, below = ((me + 1) % nspace, rep), ((me + nspace - 1) % nspace, rep)
    partners = at.sum_partners() + [above, below]
    barrier = pltpu.get_barrier_semaphore()
    for partner in partners:
        pl.semaphore_signal(barrier, inc=1, device_id=partner, device_id_type=MESH)
    loads = [pltpu.make_async_copy(src, dst, load_sem.at[i])
             for i, (src, dst) in enumerate(zip(held, loaded))]
    for load in loads:
        load.start()

    def link(slot, src, dst, device):
        return pltpu.make_async_remote_copy(
            src_ref=src, dst_ref=dst, send_sem=pair_send.at[slot], recv_sem=pair_recv.at[slot],
            device_id=device, device_id_type=MESH)

    started = []

    def send(slot, src, dst, device):
        copy = link(slot, src, dst, device)
        copy.start()
        started.append(copy)

    for load in loads[:5]:
        load.wait()
    occ = occupancy[...].astype(BF16)
    for j in range(BRICKS):
        source[j] = features[j] * occ[j:j + 1]
    source[BRICKS] = jnp.zeros((FINE, 512), BF16)
    upper[BRICKS] = jnp.zeros((FINE, 128), BF16)
    lower[BRICKS] = jnp.zeros((FINE, 128), BF16)
    owner_of = [owners[j] % NY for j in range(BRICKS)]

    def brick_for(member):
        found = BRICKS
        for j in range(BRICKS):
            found = jnp.where(owner_of[j] == member, j, found)
        return found

    for k in range(NY):
        member = (at.y + k) % NY
        label = -1
        for j in range(BRICKS):
            label = jnp.where(owner_of[j] == member, octslots[j], label)
        lab_out[k] = jnp.full((8, 128), label, jnp.int32)

    grads[(SUB_BLOCKS - 1) * SUB_ROWS:DOWN_START] = jnp.zeros((SUB_ROWS, 128), F32)
    grads[USED_ROWS:] = jnp.zeros((grads.shape[0] - USED_ROWS, 128), F32)

    def own_planes(bricks):
        for j in bricks:
            for n in range(9):
                which = jnp.clip(neighbours[j, 9 + n] - BRICKS, 0, BRICKS)
                for p in range(4):
                    row = (j * 4 + p) * FINE
                    gathered[row:row + FINE, n * 128:(n + 1) * 128] = (
                        source[which, :, p * 128:(p + 1) * 128])
        start = bricks[0] * 4 * FINE
        planes = mul(gathered[start:start + len(bricks) * 4 * FINE], pad_m[...]).astype(BF16)
        planes = mul(planes, tap_m[...]).astype(BF16)
        for j in bricks:
            for p in range(4):
                row, column = (j * 4 + p) * FINE - start, j * PLANES + p * 128
                for t in range(TAPS):
                    window[t * FINE:(t + 1) * FINE, column:column + 128] = (
                        planes[row:row + FINE, t * 128:(t + 1) * 128])

    for load in loads[5:7]:
        load.wait()
    own_planes(range(2))
    pl.semaphore_wait(barrier, len(partners))
    own, head, tail = pl.ds(0, BRICKS), pl.ds(0, 128), pl.ds(384, 128)
    for k in far_first(NY):
        send(1 + k, lab_out.at[k], lab_in.at[k], at.along_y(k))
    send(0, source.at[own, :, tail], lower.at[own], above)
    send(1, source.at[own, :, head], upper.at[own], below)
    lab_in[0] = lab_out[0]

    own_planes(range(2, BRICKS))
    for load in loads[7:]:
        load.wait()
    spread = mul(cotangent[...].reshape(2 * COARSE, 512), place_m[...], NT)
    for s in range(2):
        for m in range(8):
            block = spread[s * COARSE:(s + 1) * COARSE, m * 128:(m + 1) * 128]
            table[8 * s + m] = packed(block).astype(BF16)
    for kx in range(3):
        w_cat[kx * FINE:(kx + 1) * FINE] = jnp.concatenate(
            [w_sub[TAPS * kx + t] for t in range(TAPS)], axis=1)
    for pair in range(4):
        for parity in range(2):
            w_pair[pair * FINE:(pair + 1) * FINE, parity * 128:(parity + 1) * 128] = (
                w_down[2 * pair + parity])

    for k in [0] + near_first(NY):
        if k:
            link(1 + k, lab_out.at[k], lab_in.at[k], at.along_y(-k)).wait_recv()
        labels = lab_in[k]
        answer = chosen(labels, 0, table[0])
        for slot in range(1, 16):
            answer = answer + chosen(labels, slot, table[slot])
        if k:
            rep_out[k] = answer
            send(8 + k, rep_out.at[k], rep_in.at[k], at.along_y(-k))
        else:
            rep_in[0] = answer

    link(0, source.at[own, :, tail], lower.at[own], below).wait_recv()
    link(1, source.at[own, :, head], upper.at[own], above).wait_recv()
    low = low_lanes((FINE, 128))
    for j in range(BRICKS):
        for n in range(9):
            which_low = jnp.clip(neighbours[j, n], 0, BRICKS)
            which_high = jnp.clip(neighbours[j, 18 + n] - 2 * BRICKS, 0, BRICKS)
            edge[j * FINE:(j + 1) * FINE, n * 128:(n + 1) * 128] = jnp.where(
                low, upper[which_high], lower[which_low])
    planes = mul(edge[...], pad_m[...]).astype(BF16)
    planes = mul(planes, tap_m[...]).astype(BF16)
    for j in range(BRICKS):
        column = j * PLANES + 512
        for t in range(TAPS):
            window[t * FINE:(t + 1) * FINE, column:column + 128] = (
                planes[j * FINE:(j + 1) * FINE, t * 128:(t + 1) * 128])

    def turned(rows):
        return [pltpu.roll(rows[:, i * 128:(i + 1) * 128], 64, 1) for i in range(rows.shape[1] // 128)]

    for two in range(BRICKS // 2):
        columns = slice(2 * two * PLANES, 2 * (two + 1) * PLANES)
        wide = mul(w_cat[...], window[:, columns])
        for j in (2 * two, 2 * two + 1):
            brick = wide[:, j % 2 * PLANES:(j % 2 + 1) * PLANES]
            behind, ahead = turned(brick[:FINE]), turned(brick[2 * FINE:])
            for i in range(4):
                lanes = slice(i * 128, (i + 1) * 128)
                total = brick[FINE:2 * FINE, lanes]
                total = total + jnp.where(low, ahead[i], ahead[i + 1])
                total = total + jnp.where(low, behind[i - 1], behind[i])
                pre_act = total * occupancy[j:j + 1, lanes].astype(F32)
                active[j * FINE:(j + 1) * FINE, lanes] = jnp.maximum(pre_act, 0.0).astype(BF16)

    octants = mul(active[...], oct_m[...]).astype(BF16)
    for j in range(BRICKS):
        for pair in range(4):
            act_oct[pair * FINE:(pair + 1) * FINE, j * 128:(j + 1) * 128] = (
                octants[j * FINE:(j + 1) * FINE, pair * 128:(pair + 1) * 128])
    summed = mul(w_pair[...], act_oct[...], TN)
    for j in range(BRICKS):
        even = summed[:COARSE, j * 128:(j + 1) * 128]
        odd = summed[COARSE:, j * 128:(j + 1) * 128]
        both = jnp.where(low_lanes((COARSE, 128)), even, odd)
        both = both + pltpu.roll(both, 64, 1)
        oct_pack[j] = packed(both).astype(BF16)
    oct_pack[BRICKS] = jnp.zeros((64, 128), BF16)
    for k in far_first(NY) + [0]:
        block = oct_pack[brick_for((at.y + k) % NY)]
        if k:
            oct_out[k] = block
            send(15 + k, oct_out.at[k], oct_in.at[k], at.along_y(k))
        else:
            oct_in[0] = block

    for k in range(1, NY):
        link(8 + k, rep_out.at[k], rep_in.at[k], at.along_y(k)).wait_recv()
    low_rows = low_lanes((64, 128))
    for j in range(BRICKS):
        block = rep_in[(owner_of[j] - at.y + NY) % NY].astype(F32)
        other = pltpu.roll(block, 64, 1)
        returned[0:64, j * 128:(j + 1) * 128] = jnp.where(low_rows, block, other).astype(BF16)
        returned[64:128, j * 128:(j + 1) * 128] = jnp.where(low_rows, other, block).astype(BF16)
    whole = returned[...].astype(F32)
    low_half = low_lanes((COARSE, 512))
    ret_half[:COARSE] = jnp.where(low_half, whole, 0.0).astype(BF16)
    ret_half[COARSE:] = jnp.where(low_half, 0.0, whole).astype(BF16)
    spread = mul(w_down[...].reshape(8 * FINE, COARSE), returned[...])
    low_half = low_lanes((FINE, 512))
    for pair in range(4):
        even = spread[2 * pair * FINE:(2 * pair + 1) * FINE]
        odd = spread[(2 * pair + 1) * FINE:(2 * pair + 2) * FINE]
        both = jnp.where(low_half, even, odd).astype(BF16)
        for j in range(BRICKS):
            back[j * FINE:(j + 1) * FINE, pair * 128:(pair + 1) * 128] = both[:, j * 128:(j + 1) * 128]
    grad_act = mul(back[...], oct_m[...], NT)
    grad_pre = jnp.where(active[...].astype(F32) > 0, grad_act, 0.0)
    for j in range(BRICKS):
        brick = grad_pre[j * FINE:(j + 1) * FINE]
        sides = turned(brick) + [jnp.zeros((FINE, 128), F32)]
        for i in range(5):
            lanes = slice(j * PLANES + i * 128, j * PLANES + (i + 1) * 128)
            middle = brick[:, i * 128:(i + 1) * 128] if i < 4 else sides[4]
            shifted[0:FINE, lanes] = jnp.where(low, sides[i], sides[(i + 1) % 5]).astype(BF16)
            shifted[FINE:2 * FINE, lanes] = middle.astype(BF16)
            shifted[2 * FINE:, lanes] = jnp.where(low, sides[i - 1], sides[i]).astype(BF16)

    part = mul(act_oct[...], ret_half[...], NT)
    for parity in range(2):
        start = DOWN_START + parity * DOWN_ROWS
        grads[start:start + DOWN_ROWS] = part[:, parity * 128:(parity + 1) * 128]
    part = mul(shifted[...], window[...], NT)
    for b in range(SUB_BLOCKS):
        width = min(128, TAPS * FINE - b * 128)
        grads[b * SUB_ROWS:(b + 1) * SUB_ROWS, 0:width] = part[:, b * 128:b * 128 + width]
    work.start()

    def place_octants():
        for k in range(1, NY):
            link(15 + k, oct_out.at[k], oct_in.at[k], at.along_y(-k)).wait_recv()
        for slot in range(16):
            s, m = slot // 8, slot % 8
            block = chosen(lab_in[0], slot, oct_in[0])
            for k in range(1, NY):
                block = block + chosen(lab_in[k], slot, oct_in[k])
            block = block.astype(F32)
            lanes = slice(m * 128, (m + 1) * 128)
            place_in[s * 128:s * 128 + 64, lanes] = jnp.where(low_rows, block, 0.0).astype(BF16)
            place_in[s * 128 + 64:s * 128 + 128, lanes] = jnp.where(low_rows, 0.0, block).astype(BF16)
        result = mul(place_in[...], place_m[...]).astype(BF16)
        for s in range(2):
            coarse[s] = result[s * COARSE:(s + 1) * COARSE]

    save = pltpu.make_async_copy(coarse, out_coarse, load_sem.at[len(loads)])
    def while_waiting():
        place_octants()
        save.start()

    work.sent += started
    work.run(while_waiting)
    work.finish()
    save.wait()


def unpack_kernel(total, coarse_in, coarse, grad_sub, grad_down, sub, down, sems):
    copies = [pltpu.make_async_copy(coarse_in, coarse, sems.at[0])]
    copies[0].start()
    for octant in range(8):
        row = DOWN_START + octant % 2 * DOWN_ROWS + octant // 2 * FINE
        down[octant] = total[row:row + FINE].astype(F32)
    copies.append(pltpu.make_async_copy(down, grad_down, sems.at[1]))
    copies[-1].start()

    def block(b, kx):
        row = b * SUB_ROWS + kx * FINE
        return total[row:row + FINE].astype(F32)

    lane = lax.broadcasted_iota(jnp.int32, (FINE, 128), 1)
    for kx in range(3):
        for t in range(TAPS):
            b, offset = t * FINE // 128, t * FINE % 128
            left = block(b, kx)
            if offset:
                left = pltpu.roll(left, 128 - offset, 1)
            if offset > 32:
                right = pltpu.roll(block(b + 1, kx), 128 - offset, 1)
                left = jnp.where(lane < 128 - offset, left, right)
            sub[TAPS * kx + t] = left[:, :FINE]
        taps = pl.ds(TAPS * kx, TAPS)
        copies.append(pltpu.make_async_copy(sub.at[taps], grad_sub.at[taps], sems.at[2 + kx]))
        copies[-1].start()
    for copy in copies:
        copy.wait()


def per_device(sizes, features, occupancy, neighbours, owners, octslots, cotangent, w_sub, w_down):
    vmem = pl.BlockSpec(memory_space=pltpu.VMEM)
    hbm = pl.BlockSpec(memory_space=pl.ANY)
    v = pltpu.VMEM
    held = [neighbours[0], owners[0], octslots[0], features[0], occupancy[0], jnp.asarray(padding_matrix()), jnp.asarray(tap_matrix()),
            cotangent[0], jnp.asarray(placing_matrix()), w_sub, jnp.transpose(w_down, (0, 2, 1)),
            jnp.asarray(octant_matrix())]
    total, coarse = pl.pallas_call(
        functools.partial(kernel, sizes),
        out_shape=(
            jax.ShapeDtypeStruct((2 * sizes[1] * SHARE, 128), BF16),
            jax.ShapeDtypeStruct(cotangent.shape[1:], BF16),
        ),
        in_specs=[hbm] * 12,
        out_specs=(hbm, hbm),
        scratch_shapes=[pltpu.SMEM(a.shape, a.dtype) for a in held[:3]] + [
            v(a.shape, a.dtype) for a in held[3:]] + [
            pltpu.SemaphoreType.DMA((13,)),
            v((BRICKS + 1, FINE, 512), BF16),
            v((BRICKS + 1, FINE, 128), BF16),
            v((BRICKS + 1, FINE, 128), BF16),
            v((BRICKS * 4 * FINE, TAPS * 128), BF16),
            v((BRICKS * FINE, TAPS * 128), BF16),
            v((TAPS * FINE, BRICKS * PLANES), BF16),
            v((BRICKS * FINE, 512), BF16),
            v((4 * FINE, BRICKS * 128), BF16),
            v((3 * FINE, TAPS * FINE), BF16),
            v((4 * FINE, 2 * COARSE), BF16),
            v((BRICKS + 1, 64, 128), BF16),
            v((NY, 64, 128), BF16),
            v((NY, 64, 128), BF16),
            v((NY, 8, 128), jnp.int32),
            v((NY, 8, 128), jnp.int32),
            v((16, 64, 128), BF16),
            v((NY, 64, 128), BF16),
            v((NY, 64, 128), BF16),
            v((COARSE, BRICKS * 128), BF16),
            v((2 * COARSE, BRICKS * 128), BF16),
            v((BRICKS * FINE, 512), BF16),
            v((3 * FINE, BRICKS * PLANES), BF16),
            v((2 * COARSE, 1024), BF16),
            v((2, COARSE, 512), BF16),
            pltpu.SemaphoreType.DMA((2 + 3 * (NY - 1),)),
            pltpu.SemaphoreType.DMA((2 + 3 * (NY - 1),)),
        ] + sum_scratch(sizes[1]),
        compiler_params=pltpu.CompilerParams(
            collective_id=0, has_side_effects=True, vmem_limit_bytes=56 * 2**20
        ),
    )(*held)
    coarse, grad_sub, grad_down = pl.pallas_call(
        unpack_kernel,
        out_shape=(
            jax.ShapeDtypeStruct(cotangent.shape[1:], BF16),
            jax.ShapeDtypeStruct(w_sub.shape, F32),
            jax.ShapeDtypeStruct((8, FINE, COARSE), F32),
        ),
        in_specs=[vmem, vmem],
        out_specs=(hbm, hbm, hbm),
        scratch_shapes=[
            v(w_sub.shape, F32),
            v((8, FINE, COARSE), F32),
            pltpu.SemaphoreType.DMA((5,)),
        ],
        compiler_params=pltpu.CompilerParams(vmem_limit_bytes=56 * 2**20),
    )(total, coarse)
    return coarse[None], grad_sub, jnp.transpose(grad_down, (0, 2, 1))


def solution(mesh):
    sizes = (mesh.shape["space"] // NY, mesh.shape["rep"] // 2)
    return jax.shard_map(
        functools.partial(per_device, sizes),
        mesh=mesh,
        in_specs=(
            P("rep", "space", None, None),
            P("rep", "space", None),
            P("rep", "space", None),
            P("rep", "space"),
            P("rep", "space"),
            P("rep", "space", None, None),
            P(),
            P(),
        ),
        out_specs=(P("rep", "space", None, None), P(), P()),
        check_vma=False,
    )
```
